128 devices in a mesh: row: 4 (over x), col: 32 (over z, y, core).
Axes of the slice: x: 4, y: 4, z: 4, core: 2. Of those that a mesh axis runs over, the one named last changes fastest.
Arguments:
- tokens: bfloat16 [112, 896, 768], P('row', 'col'), may hold values from -6 to 6
- project_in: bfloat16 [768, 2304], replicated, may hold values from -8 to 8
- project_out: bfloat16 [768, 768], replicated, may hold values from -0.21875 to 0.21875
- expand_weight: bfloat16 [768, 3072], replicated, may hold values from -0.21875 to 0.21875
- reduce_weight: bfloat16 [3072, 768], replicated, may hold values from -0.109375 to 0.109375
- first_weight: bfloat16 [49, 768, 1024], P(None, 'row', 'col'), may hold values from -0.03125 to 0.03125
- first_bias: float32 [1024], replicated, may hold values from -3 to 3
- second_weight: bfloat16 [1024, 1024], replicated, may hold values from -0.1875 to 0.1875
- second_bias: float32 [1024], replicated, may hold values from -3 to 3
- box_tile: int32 [4096, 1], replicated, may hold values from 0 to 127; in each aligned block of 128 rows (0 to 127, 128 to 255, ...) at most 2 rows name the same one
- box_shape: int32 [4096, 4], replicated, may hold values from 0 to 7, as said below
Outputs:
- features: bfloat16 [112, 896, 768], P('row', 'col')
- box_features: bfloat16 [4096, 1024], P('col', 'row')
The draws below stay inside these ranges and needn't reach their ends.
Inputs may be any that keep to these rules, and one draw needn't show every extreme that they name: `box_tile`: among the 128 boxes of one aligned block (boxes b * 128 to (b + 1) * 128 - 1), no tile is named more than 2 times, a bound that some block reaches; every tile holds some box. `box_shape`: steps are 1 or 2, and first + 6 step < 14 in both directions, so all samples of a box lie in its tile.
All inputs are finite; a program needn't handle non-finite values.
Results may differ from the reference program's by a relative error of at most 0.02.
Values may be sent and summed in bfloat16 or wider, within the bound.
A program may use at most 192 MiB of HBM per device.

```python
import math
import jax
import jax.numpy as jnp
import numpy as np
from jax import lax

D = 768
HEADS = 12
MLP = 3072
FC = 1024
WIN = 14
POOL = 7
HEAD_DIM = 64
BINS = 49
PH = 14
BAND_H = 112
BAND_W = 896
BOX_COL = 128
BOXES = 4096
CAP = 2
N_COL = 32
DEVICES = 128


def draw_project_in(key, part):
    key = jax.random.fold_in(key, 3)
    normal_key = jax.random.fold_in(key, 0)
    matrix = jax.random.normal(normal_key, (D, 3 * D), jnp.float32) * D ** (-0.5)
    return matrix.astype(jnp.bfloat16)


def draw_box_shape(key, part):
    key = jax.random.fold_in(key, 7)
    subkeys = jax.random.split(key, 4)
    row_index = jnp.arange(BOXES, dtype=jnp.int32)
    border = row_index % 16 == 0
    row_step = jax.random.randint(subkeys[0], (BOXES,), 1, 3)
    col_step = jax.random.randint(subkeys[1], (BOXES,), 1, 3)
    row_step = jnp.where(border, 1, row_step)
    row_first = jax.random.randint(subkeys[2], (BOXES,), 0, PH - 6 * row_step)
    col_first = jax.random.randint(subkeys[3], (BOXES,), 0, PH - 6 * col_step)
    row_first = jnp.where(border, PH - 7, row_first)
    col_first = jnp.where(row_index % 16 == 1, 0, col_first)
    return jnp.stack([row_first, col_first, row_step, col_step], axis=1).astype(jnp.int32)


def level_of(own_key, extent, cuts, low, largest):
    def one(dim, blocks):
        heights = jax.random.uniform(jax.random.fold_in(jax.random.fold_in(own_key, 6), dim), (blocks,), jnp.float32, low / len(cuts), largest / len(cuts))
        return jnp.repeat(jnp.exp(heights), extent[dim] // blocks).reshape((-1,) + (1,) * (len(extent) - dim - 1))

    level = one(*cuts[0])
    for cut in cuts[1:]:
        level = level * one(*cut)
    return level


def deal_out(key, own, number, rows, amount, top, most, slope):
    order = jax.random.permutation(key, amount)
    packed, common = portions_of(amount, rows * top, most, slope, True), portions_of(amount, rows * top, most, slope, False)
    places = jnp.arange(amount)

    def named(tallies, turn):
        used = int((tallies > 0).sum())
        fixed = max(1, used // 4)
        shifted = fixed + (places - fixed + turn * (used - fixed)) % max(1, amount - fixed)
        return jnp.zeros((amount,), jnp.int32).at[order[jnp.where(places < fixed, places, shifted)]].set(jnp.asarray(tallies, jnp.int32))

    tallies = jnp.where(number % 4 == 0, named(packed, number // 4), named(common, number - number // 4 - 1))
    mixed = jax.random.permutation(jax.random.fold_in(own, 3), amount)
    donor, taker = mixed[0:amount // 2 * 2:2], mixed[1:amount // 2 * 2:2]
    room = jnp.minimum(tallies[donor] - 1, most - tallies[taker]) // 2
    room = jnp.where((donor == order[0]) | (taker == order[0]) | (tallies[taker] == 0), 0, jnp.maximum(room, 0))
    shifted = jax.random.randint(jax.random.fold_in(own, 4), (amount // 2,), 0, 1 << 20) % (room + 1)
    tallies = tallies.at[donor].add(-shifted).at[taker].add(shifted)
    items = jnp.searchsorted(jnp.cumsum(tallies), jnp.arange(rows * top), side="right").astype(jnp.int32)
    listing = items.reshape(top, rows).T
    listing = listing[jax.random.permutation(jax.random.fold_in(own, 1), rows)]
    turn = jax.random.randint(jax.random.fold_in(own, 2), (rows, 1), 0, top)
    return jnp.take_along_axis(listing, (jnp.arange(top)[None, :] + turn) % top, axis=1)


def portions_of(amount, total, bound, lean, full):
    portions = [(1 << 20) // math.isqrt(standing ** lean) + 1 for standing in range(1, amount + 1)]
    largest = bound if full else min(bound, max(-(-total // amount), total * portions[0] // sum(portions)))
    least = 1 if total - largest >= amount - 1 else 0
    given, surplus = [largest] + [least] * (amount - 1), total - largest - least * (amount - 1)
    while surplus > 0:
        movable = [i for i in range(1, amount) if given[i] < largest] or [i for i in range(1, amount) if given[i] < bound]
        pool, remaining = sum([portions[i] for i in movable]), surplus
        for i in movable:
            addition = min(bound - given[i], max(1, remaining * portions[i] // pool), surplus)
            given[i] = given[i] + addition
            surplus = surplus - addition
    return np.array(given)


def normal_values(own_key, shape, width, reach, cuts=(), kind=jnp.bfloat16):
    values = width * jax.random.normal(own_key, shape, jnp.float32)
    if cuts:
        values = values * level_of(own_key, shape, cuts, -0.22, 0.18)
    return jnp.clip(values, -reach, reach).astype(kind)


def setup_inputs(seed: int = 0) -> dict:
    arg_keys = jax.random.split(jax.random.key(seed), 12)
    tokens = normal_values(arg_keys[0], (BAND_H, BAND_W, D), 1.0, 6.0, ((0, 4), (1, 32)))
    project_in = draw_project_in(jax.random.fold_in(arg_keys[11], 71), 0)
    project_out = normal_values(arg_keys[2], (D, D), D ** -0.5, 0.21875)
    expand_weight = normal_values(arg_keys[3], (D, MLP), D ** -0.5, 0.21875)
    reduce_weight = normal_values(arg_keys[4], (MLP, D), MLP ** -0.5, 0.109375)
    first_weight = normal_values(arg_keys[5], (BINS, D, FC), (BINS * D) ** -0.5, 0.03125, ((1, 4), (2, 32)))
    first_bias = normal_values(arg_keys[6], (FC,), 0.5, 3.0, (), jnp.float32)
    second_weight = normal_values(arg_keys[7], (FC, FC), FC ** -0.5, 0.1875)
    second_bias = normal_values(arg_keys[8], (FC,), 0.5, 3.0, (), jnp.float32)
    box_tile_keys = jax.random.split(jax.random.fold_in(arg_keys[9], 1), BOXES // BOX_COL)
    box_tile_turns = jax.random.permutation(jax.random.fold_in(arg_keys[9], 3), BOXES // BOX_COL)
    box_tile = jax.vmap(lambda own, number: deal_out(jax.random.fold_in(arg_keys[9], 2), own, number, BOX_COL, DEVICES, 1, CAP, 2))(box_tile_keys, box_tile_turns).reshape((BOXES, 1))
    box_shape = draw_box_shape(jax.random.fold_in(arg_keys[11], 71), 0)
    return dict(tokens=tokens, project_in=project_in, project_out=project_out, expand_weight=expand_weight, reduce_weight=reduce_weight, first_weight=first_weight, first_bias=first_bias, second_weight=second_weight, second_bias=second_bias, box_tile=box_tile, box_shape=box_shape)


eps = 1e-06
masked = -1e+30

def layer_norm(values):
    values = values.astype(jnp.float32)
    center = values - lax.optimization_barrier(jnp.mean(values, axis=-1, keepdims=True))
    spread = lax.optimization_barrier(jnp.mean(center * center, axis=-1, keepdims=True))
    return (center * lax.rsqrt(spread + eps)).astype(jnp.bfloat16)

def to_windows(lattice, window):
    side_rows, side_cols, channels = lattice.shape
    row_blocks = side_rows // window
    col_blocks = side_cols // window
    shaped = lattice.reshape(row_blocks, window, col_blocks, window, channels)
    return shaped.transpose(0, 2, 1, 3, 4).reshape(row_blocks * col_blocks, window * window, channels)

def from_windows(blocks, row_blocks, col_blocks, window):
    channels = blocks.shape[-1]
    shaped = blocks.reshape(row_blocks, col_blocks, window, window, channels)
    return shaped.transpose(0, 2, 1, 3, 4).reshape(row_blocks * window, col_blocks * window, channels)

def attend(queries, key_value, inside):
    window_count = queries.shape[0]
    length = queries.shape[1]
    query_heads = queries.astype(jnp.float32).reshape(window_count, length, HEADS, HEAD_DIM)
    key_heads = key_value[..., :D].astype(jnp.float32).reshape(window_count, length, HEADS, HEAD_DIM)
    value_heads = key_value[..., D:].astype(jnp.float32).reshape(window_count, length, HEADS, HEAD_DIM)
    scores = jnp.einsum('nqhd,nkhd->nhqk', query_heads, key_heads) * HEAD_DIM ** (-0.5)
    scores = jnp.where(inside[:, None, None, :], scores, masked)
    row_max = lax.optimization_barrier(jnp.max(scores, axis=-1, keepdims=True))
    weights = jnp.exp(scores - row_max)
    shares = (weights / lax.optimization_barrier(jnp.sum(weights, axis=-1, keepdims=True))).astype(jnp.bfloat16)
    blended = jnp.einsum('nhqk,nkhd->nqhd', shares.astype(jnp.float32), value_heads)
    return blended.reshape(window_count, length, D).astype(jnp.bfloat16)

def finish(tokens_flat, blended, project_out, expand_weight, reduce_weight):
    after_attention = tokens_flat.astype(jnp.float32) + jnp.dot(blended, project_out, preferred_element_type=jnp.float32)
    hidden = jax.nn.gelu(jnp.dot(layer_norm(after_attention), expand_weight, preferred_element_type=jnp.float32)).astype(jnp.bfloat16)
    return (after_attention + jnp.dot(hidden, reduce_weight, preferred_element_type=jnp.float32)).astype(jnp.bfloat16)

def reference(tokens, project_in, project_out, expand_weight, reduce_weight, first_weight, first_bias, second_weight, second_bias, box_tile, box_shape):
    margin = WIN // 2
    padded = jnp.pad(tokens, ((margin, margin), (margin, margin), (0, 0)))
    strip_width = BAND_W + WIN
    col_coord = jnp.arange(strip_width, dtype=jnp.int32) - margin
    col_inside = (col_coord >= 0) & (col_coord < BAND_W)

    def one_strip(strip_index):
        strip = lax.dynamic_slice_in_dim(padded, strip_index * WIN, WIN, 0)
        row_coord = strip_index * WIN + jnp.arange(WIN, dtype=jnp.int32) - margin
        inside = ((row_coord >= 0) & (row_coord < BAND_H))[:, None] & col_inside[None, :]
        normed = layer_norm(strip.reshape(-1, D))
        projected = jnp.dot(normed, project_in, preferred_element_type=jnp.float32).astype(jnp.bfloat16)
        windows = to_windows(projected.reshape(WIN, strip_width, 3 * D), WIN)
        inside_flat = to_windows(inside[:, :, None], WIN)[..., 0]
        blended = attend(windows[..., :D], windows[..., D:], inside_flat)
        blended = from_windows(blended, 1, strip_width // WIN, WIN).reshape(-1, D)
        result = finish(strip.reshape(-1, D), blended, project_out, expand_weight, reduce_weight)
        return result.reshape(WIN, strip_width, D)
    strips = lax.map(one_strip, jnp.arange(BAND_H // WIN + 1, dtype=jnp.int32))
    features = strips.reshape(-1, strip_width, D)[margin:margin + BAND_H, margin:margin + BAND_W]
    pooled = (features.astype(jnp.float32).reshape(BAND_H // 2, 2, BAND_W // 2, 2, D).sum(axis=(1, 3)) * 0.25).astype(jnp.bfloat16)
    pooled_flat = pooled.reshape(-1, D)
    anchor = box_tile[:, 0]
    offsets = jnp.arange(POOL, dtype=jnp.int32)
    row_start = anchor // N_COL * PH + box_shape[:, 0]
    col_start = anchor % N_COL * PH + box_shape[:, 1]
    sample_rows = row_start[:, None] + offsets[None, :] * box_shape[:, 2:3]
    sample_cols = col_start[:, None] + offsets[None, :] * box_shape[:, 3:4]
    sample_at = (sample_rows[:, :, None] * (BAND_W // 2) + sample_cols[:, None, :]).reshape(N_COL, BOX_COL, BINS)
    flat_weight = first_weight.reshape(BINS * D, FC)

    def first_layer(block_index):
        crop_bins = pooled_flat[block_index.reshape(-1)].reshape(-1, BINS * D)
        return jnp.dot(crop_bins, flat_weight, preferred_element_type=jnp.float32)
    first_sum = lax.map(first_layer, sample_at).reshape(BOXES, FC)
    box_hidden = jax.nn.relu(first_sum + first_bias).astype(jnp.bfloat16)
    second_sum = jnp.dot(box_hidden, second_weight, preferred_element_type=jnp.float32)
    box_features = jax.nn.relu(second_sum + second_bias).astype(jnp.bfloat16)
    return (features, box_features)
```

```python
import functools

import jax
import jax.numpy as jnp
from jax import lax
from jax.experimental import pallas as pl
from jax.experimental.pallas import tpu as pltpu
from jax.sharding import PartitionSpec as P

ROWS = 4
COLS = 32
D = 768
SIDE = 28
HEADS = 12
MLP = 3072
FC = 1024
S0, S1, S2, OWN = 0, 224, 672, 896
TOP, BOT, LEFT, RIGHT, TL, TR, BL, BR, HALO = 0, 240, 480, 704, 928, 992, 1056, 1120, 1184
HALO_COPIES = (
    (S0 + 160, 64, TOP, 1, 0),
    (S1 + 336, 112, TOP + 64, 1, 0),
    (S2 + 160, 64, TOP + 176, 1, 0),
    (S0, 64, BOT, -1, 0),
    (S1, 112, BOT + 64, -1, 0),
    (S2, 64, BOT + 176, -1, 0),
    (S2, 224, LEFT, 0, 1),
    (S0, 224, RIGHT, 0, -1),
    (S2 + 160, 64, TL, 1, 1),
    (S0 + 160, 64, TR, 1, -1),
    (S2, 64, BL, -1, 1),
    (S0, 64, BR, -1, -1),
)
MESH = pl.DeviceIdType.MESH
F32 = jnp.float32
BF16 = jnp.bfloat16
VMEM_SPEC = pl.BlockSpec(memory_space=pltpu.VMEM)


def greet(peers):
    barrier = pltpu.get_barrier_semaphore()
    for peer in peers:
        pl.semaphore_signal(barrier, inc=1, device_id=peer, device_id_type=MESH)
    pl.semaphore_wait(barrier, len(peers))


def halo_kernel(tokens_ref, own_ref, halo_ref, wide_ref, send_sem, recv_sem):
    row, col = lax.axis_index("row"), lax.axis_index("col")

    def near(dr, dc):
        return lax.rem(row + dr + ROWS, ROWS), lax.rem(col + dc + COLS, COLS)

    barrier = pltpu.get_barrier_semaphore()
    peers = [near(dr, dc) for dr in (-1, 0, 1) for dc in (-1, 0, 1) if (dr, dc) != (0, 0)]
    for peer in peers:
        pl.semaphore_signal(barrier, inc=1, device_id=peer, device_id_type=MESH)
    for y in range(0, SIDE, 2):
        for a in range(2):
            wide_ref[a, 0:SIDE, :] = tokens_ref[y + a].astype(F32)
        own_ref[S0 + y * 8 : S0 + y * 8 + 16, :] = jnp.concatenate(
            [wide_ref[a, 0:8, :] for a in range(2)], axis=0
        ).astype(BF16)
        own_ref[S1 + y * 16 : S1 + y * 16 + 32, :] = jnp.concatenate(
            [wide_ref[a, 7:23, :] for a in range(2)], axis=0
        ).astype(BF16)
        own_ref[S2 + y * 8 : S2 + y * 8 + 16, :] = jnp.concatenate(
            [wide_ref[a, 20:28, :] for a in range(2)], axis=0
        ).astype(BF16)
    pl.semaphore_wait(barrier, len(peers))
    copies = [
        pltpu.make_async_remote_copy(
            src_ref=own_ref.at[pl.ds(src, rows)],
            dst_ref=halo_ref.at[pl.ds(dst, rows)],
            send_sem=send_sem.at[n],
            recv_sem=recv_sem.at[n],
            device_id=near(dr, dc),
            device_id_type=MESH,
        )
        for n, (src, rows, dst, dr, dc) in enumerate(HALO_COPIES)
    ]
    for copy in copies:
        copy.start()
    for copy in copies:
        copy.wait()


def exchange_halo(tokens):
    return pl.pallas_call(
        halo_kernel,
        out_shape=(
            jax.ShapeDtypeStruct((OWN, D), BF16),
            jax.ShapeDtypeStruct((HALO, D), BF16),
        ),
        in_specs=[VMEM_SPEC],
        out_specs=(VMEM_SPEC, VMEM_SPEC),
        scratch_shapes=[
            pltpu.VMEM((2, 32, D), F32),
            pltpu.SemaphoreType.DMA((len(HALO_COPIES),)),
            pltpu.SemaphoreType.DMA((len(HALO_COPIES),)),
        ],
        compiler_params=pltpu.CompilerParams(collective_id=0, has_side_effects=True),
        name="halo",
    )(tokens)


def norm(values):
    center = values - jnp.mean(values, axis=-1, keepdims=True)
    spread = jnp.mean(center * center, axis=-1, keepdims=True)
    return (center * lax.rsqrt(spread + 1e-6)).astype(BF16)


def window_sources():
    strips = {
        "s0": (S0, 8, (TOP, 8), (BOT, 0), False),
        "s1": (S1, 16, (TOP + 64, 0), (BOT + 64, 0), False),
        "s2": (S2, 8, (TOP + 176, 8), (BOT + 176, 0), False),
        "l": (LEFT, 8, (TL, 8), (BL, 0), True),
        "r": (RIGHT, 8, (TR, 8), (BR, 0), True),
    }
    windows = []
    for wy in range(3):
        for names in (("s0", "l"), ("s1",), ("s2", "r")):
            pieces = []
            for name in names:
                base, cells, top, bottom, outer = strips[name]
                if wy == 0:
                    pieces.append((True, top[0], top[1], 7 * cells))
                    pieces.append((outer, base, 0, 7 * cells))
                elif wy == 1:
                    pieces.append((outer, base + 7 * cells, 0, 14 * cells))
                else:
                    pieces.append((outer, base + 21 * cells, 0, 7 * cells))
                    pieces.append((True, bottom[0], bottom[1], 7 * cells))
            windows.append(pieces)
    return windows


QUERY_ROWS = [
    ((S0, 56), (S1, 112), (S2, 56)),
    ((S0 + 56, 112), (S1 + 112, 224), (S2 + 56, 112)),
    ((S0 + 168, 56), (S1 + 336, 112), (S2 + 168, 56)),
]


def block_kernel(
    own_ref,
    halo_ref,
    project_in_ref,
    project_out_ref,
    expand_ref,
    reduce_ref,
    features_ref,
    pooled_ref,
    window_ref,
    kv_ref,
    query_ref,
    mixed_ref,
    wide_ref,
    small_ref,
):
    row, col = lax.axis_index("row"), lax.axis_index("col")
    for w, pieces in enumerate(window_sources()):
        place = w * 224
        for outer, base, skip, rows in pieces:
            source = halo_ref if outer else own_ref
            start = base + skip
            low = start // 16 * 16
            high = -(-(start + rows) // 16) * 16
            values = source[low:high, :].astype(F32)
            window_ref[place : place + rows, :] = values[start - low : start - low + rows]
            place += rows

    def project(w, carry):
        at = pl.ds(pl.multiple_of(w * 224, 224), 224)
        normed = norm(window_ref[at, :])
        kv_ref[w, 0:224, :] = jnp.dot(
            normed, project_in_ref[:, D:], preferred_element_type=F32
        ).astype(BF16)
        kv_ref[w, 224:256, :] = jnp.zeros((32, 2 * D), BF16)
        return carry

    lax.fori_loop(0, 9, project, 0)

    def ask(n, carry):
        at = pl.ds(pl.multiple_of(n * 224, 224), 224)
        normed = norm(own_ref[at, :].astype(F32))
        query_ref[at, :] = (
            jnp.dot(normed, project_in_ref[:, :D], preferred_element_type=F32)
            .astype(BF16)
            .astype(F32)
            * 0.125
        )
        return carry

    lax.fori_loop(0, 4, ask, 0)

    lane = lax.broadcasted_iota(jnp.int32, (1, 256), 1)
    left_half = lax.broadcasted_iota(jnp.int32, (1, 128), 1) < 64
    for wy in range(3):
        for wx in range(3):
            w = wy * 3 + wx
            start, rows = QUERY_ROWS[wy][wx]
            eighth = lax.rem(lane, 8)
            if wx == 0:
                keep = ((lane < 112) & (eighth != 7)) | ((lane >= 112) & (eighth != 0))
                keep = keep & ((lane < 112) | (col > 0))
            elif wx == 1:
                keep = lax.rem(lane, 16) < 14
            else:
                keep = ((lane < 112) & (eighth != 0)) | ((lane >= 112) & (eighth != 7))
                keep = keep & ((lane < 112) | (col < COLS - 1))
            keep = keep & (lane < 224)
            half = lax.rem(lane, 112) < 56 if wx != 1 else lane < 112
            if wy == 0:
                keep = keep & (jnp.logical_not(half) | (row > 0))
            elif wy == 2:
                keep = keep & (half | (row < ROWS - 1))
            bias = jnp.where(keep, 0.0, -1e30).astype(F32)

            def pair(h, carry, w=w, start=start, rows=rows, bias=bias):
                first = pl.multiple_of(h * 128, 128)
                asked = query_ref[start : start + rows, pl.ds(first, 128)]
                both = jnp.concatenate(
                    [jnp.where(left_half, asked, 0.0), jnp.where(left_half, 0.0, asked)],
                    axis=0,
                ).astype(BF16)
                keys = kv_ref[w, :, pl.ds(first, 128)]
                values = kv_ref[w, :, pl.ds(pl.multiple_of(D + h * 128, 128), 128)]
                scores = (
                    lax.dot_general(
                        both, keys, (((1,), (1,)), ((), ())), preferred_element_type=F32
                    )
                    + bias
                )
                weights = jnp.exp(scores - jnp.max(scores, axis=-1, keepdims=True))
                total = jnp.sum(weights, axis=-1, keepdims=True)
                mixed = jnp.dot(weights.astype(BF16), values, preferred_element_type=F32) / total
                mixed_ref[start : start + rows, pl.ds(first, 128)] = jnp.where(
                    left_half, mixed[:rows], mixed[rows:]
                )
                return carry

            lax.fori_loop(0, HEADS // 2, pair, 0)

    def finish(n, carry):
        at = pl.ds(pl.multiple_of(n * 224, 224), 224)
        after = own_ref[at, :].astype(F32) + jnp.dot(
            mixed_ref[at, :].astype(BF16), project_out_ref[...], preferred_element_type=F32
        )
        normed = norm(after)
        total = after
        for part in range(MLP // D):
            units = slice(part * D, (part + 1) * D)
            hidden = jax.nn.gelu(
                jnp.dot(normed, expand_ref[:, units], preferred_element_type=F32)
            ).astype(BF16)
            total = total + jnp.dot(hidden, reduce_ref[units, :], preferred_element_type=F32)
        mixed_ref[at, :] = total.astype(BF16).astype(F32)
        return carry

    lax.fori_loop(0, 4, finish, 0)

    wide_ref[:, :, SIDE:, :] = jnp.zeros((6, SIDE, 32 - SIDE, 128), F32)

    def place_row(y, carry):
        for n in range(6):
            lanes = slice(n * 128, (n + 1) * 128)
            wide_ref[n, y, 0:8, :] = mixed_ref[pl.ds(pl.multiple_of(S0 + y * 8, 8), 8), lanes]
            wide_ref[n, y, 20:28, :] = mixed_ref[pl.ds(pl.multiple_of(S2 + y * 8, 8), 8), lanes]
            middle = mixed_ref[pl.ds(pl.multiple_of(S1 + y * 16, 16), 16), lanes]
            wide_ref[n, y, 7:21, :] = middle[:14]
        features_ref[y] = jnp.concatenate(
            [wide_ref[n, y, 0:SIDE, :] for n in range(6)], axis=1
        ).astype(BF16)
        return carry

    lax.fori_loop(0, SIDE, place_row, 0)

    def pool(u, carry):
        for n in range(6):
            total = (
                wide_ref[n, 2 * u, pl.ds(0, 16, stride=2), :]
                + wide_ref[n, 2 * u, pl.ds(1, 16, stride=2), :]
                + wide_ref[n, 2 * u + 1, pl.ds(0, 16, stride=2), :]
                + wide_ref[n, 2 * u + 1, pl.ds(1, 16, stride=2), :]
            )
            small_ref[pl.ds(pl.multiple_of(u * 16, 16), 16), n * 128 : (n + 1) * 128] = (
                total * 0.25
            )
        return carry

    lax.fori_loop(0, SIDE // 2, pool, 0)
    small_ref[224:256, :] = jnp.zeros((32, D), F32)
    for group, first in enumerate((0, 128, 384, 512)):
        values = small_ref[:, first : first + 256]
        if group % 2:
            values = pltpu.roll(values, 192, 1)
        pooled_ref[group] = values.astype(BF16)


def block(own, halo, project_in, project_out, expand_weight, reduce_weight):
    return pl.pallas_call(
        block_kernel,
        out_shape=(
            jax.ShapeDtypeStruct((SIDE, SIDE, D), BF16),
            jax.ShapeDtypeStruct((ROWS, 256, 256), BF16),
        ),
        in_specs=[VMEM_SPEC] * 6,
        out_specs=(VMEM_SPEC, VMEM_SPEC),
        scratch_shapes=[
            pltpu.VMEM((9 * 224, D), F32),
            pltpu.VMEM((9, 256, 2 * D), BF16),
            pltpu.VMEM((OWN, D), F32),
            pltpu.VMEM((OWN, D), F32),
            pltpu.VMEM((6, SIDE, 32, 128), F32),
            pltpu.VMEM((256, D), F32),
        ],
        compiler_params=pltpu.CompilerParams(vmem_limit_bytes=60 * 1024 * 1024),
        cost_estimate=pl.CostEstimate(
            flops=18_000_000_000, bytes_accessed=22_000_000, transcendentals=6_000_000
        ),
        name="block",
    )(own, halo, project_in, project_out, expand_weight, reduce_weight)


def swap_kernel(pooled_ref, out_ref, send_sem, recv_sem, own_sem):
    row, col = lax.axis_index("row"), lax.axis_index("col")
    base = col // 2 * 2
    me = row * 2 + col % 2
    others = [(me + n) % 8 for n in range(1, 8)]
    greet([(other // 2, base + other % 2) for other in others])
    own = pltpu.make_async_copy(pooled_ref.at[row], out_ref.at[me], own_sem)
    own.start()
    copies = [
        pltpu.make_async_remote_copy(
            src_ref=pooled_ref.at[other // 2],
            dst_ref=out_ref.at[me],
            send_sem=send_sem.at[n],
            recv_sem=recv_sem.at[n],
            device_id=(other // 2, base + other % 2),
            device_id_type=MESH,
        )
        for n, other in enumerate(others)
    ]
    for copy in copies:
        copy.start()
    own.wait()
    for copy in copies:
        copy.wait()


def swap_groups(pooled):
    return pl.pallas_call(
        swap_kernel,
        out_shape=jax.ShapeDtypeStruct((8, 256, 256), BF16),
        in_specs=[VMEM_SPEC],
        out_specs=VMEM_SPEC,
        scratch_shapes=[
            pltpu.SemaphoreType.DMA((7,)),
            pltpu.SemaphoreType.DMA((7,)),
            pltpu.SemaphoreType.DMA,
        ],
        compiler_params=pltpu.CompilerParams(collective_id=1, has_side_effects=True),
        name="swap",
    )(pooled)


def first_kernel(pooled_ref, tile_ref, code_ref, weight_ref, out_ref, code_at, crops, total):
    step = pl.program_id(0)
    col = lax.axis_index("col")

    @pl.when(step == 0)
    def _():
        lane = lax.broadcasted_iota(jnp.int32, (COLS, 128), 1)
        for t in range(8):
            tile = t // 2 * COLS + col // 2 * 2 + t % 2
            here = tile_ref[...] == tile
            first = jnp.min(jnp.where(here, lane, 127), axis=1, keepdims=True)
            last = jnp.max(jnp.where(here, lane, 0), axis=1, keepdims=True)
            for rank, pick in enumerate((first, last)):
                code = jnp.sum(jnp.where(lane == pick, code_ref[...], 0), axis=1, keepdims=True)
                code_at[t, rank * COLS : (rank + 1) * COLS, :] = jnp.broadcast_to(
                    code, (COLS, 128)
                )
        total[...] = jnp.zeros_like(total)

    spot = lax.broadcasted_iota(jnp.int32, (64, 128), 1)
    for t in range(8):
        code = code_at[t]
        down = 1 + lax.rem(code // 2, 2)
        right = 1 + lax.rem(code, 2)
        position = code // 4 + step * 16 * down
        picks = []
        for j in range(7):
            low = (position == spot).astype(F32)
            high = (position == spot + 128).astype(F32)
            picks.append(jnp.concatenate([low, high], axis=1).astype(BF16))
            position = position + right
        found = jnp.dot(
            jnp.concatenate(picks, axis=0), pooled_ref[t], preferred_element_type=F32
        ).astype(BF16)
        for j in range(7):
            crops[j, t * 64 : (t + 1) * 64, :] = found[j * 64 : (j + 1) * 64, :192]
    summed = total[...]
    for j in range(7):
        summed = summed + lax.dot_general(
            crops[j], weight_ref[j], (((1,), (1,)), ((), ())), preferred_element_type=F32
        )
    total[...] = summed

    @pl.when(step == 6)
    def _():
        to = lax.broadcasted_iota(jnp.int32, (512, 512), 0)
        source = lax.rem(to // 2, 8) * 64 + lax.rem(to, 2) * 32 + to // 16
        order = (source == lax.broadcasted_iota(jnp.int32, (512, 512), 1)).astype(F32).astype(BF16)
        out_ref[...] = jnp.dot(
            order, summed.astype(BF16), preferred_element_type=F32
        ).astype(BF16)


def first_layer(pooled, tiles, codes, weight):
    return pl.pallas_call(
        first_kernel,
        grid=(7,),
        out_shape=jax.ShapeDtypeStruct((512, 512), BF16),
        in_specs=[
            pl.BlockSpec((8, 256, 256), lambda i: (0, 0, 0)),
            pl.BlockSpec((COLS, 128), lambda i: (0, 0)),
            pl.BlockSpec((COLS, 128), lambda i: (0, 0)),
            pl.BlockSpec((7, 512, 192), lambda i: (i, 0, 0)),
        ],
        out_specs=pl.BlockSpec((512, 512), lambda i: (0, 0)),
        scratch_shapes=[
            pltpu.VMEM((8, 64, 128), jnp.int32),
            pltpu.VMEM((7, 512, 192), BF16),
            pltpu.VMEM((512, 512), F32),
        ],
        compiler_params=pltpu.CompilerParams(vmem_limit_bytes=40 * 1024 * 1024),
        cost_estimate=pl.CostEstimate(
            flops=8_000_000_000, bytes_accessed=12_000_000, transcendentals=0
        ),
        name="first_layer",
    )(pooled, tiles, codes, weight)


def head_kernel(
    sums_ref,
    tile_ref,
    first_bias_ref,
    second_ref,
    second_bias_ref,
    out_ref,
    shares,
    reduced,
    landed,
    parts,
    final,
    second_rows,
    row_send,
    row_recv,
    col_send,
    col_recv,
    last_send,
    last_recv,
    weight_sem,
):
    row, col = lax.axis_index("row"), lax.axis_index("col")
    rows_near = [lax.rem(row + n, ROWS) for n in range(1, ROWS)]
    barrier = pltpu.get_barrier_semaphore()
    for other in rows_near:
        pl.semaphore_signal(barrier, inc=1, device_id=(other, col), device_id_type=MESH)

    def greet_col(n, carry):
        pl.semaphore_signal(
            barrier, inc=1, device_id=(row, lax.rem(col + n, COLS)), device_id_type=MESH
        )
        return carry

    lax.fori_loop(1, COLS, greet_col, 0)
    loads = [
        pltpu.make_async_copy(
            second_ref.at[pl.ds(row * 256 + k * 64 + h * 32, 32)],
            second_rows.at[h, pl.ds(k * 32, 32)],
            weight_sem.at[h * 4 + k],
        )
        for h in range(2)
        for k in range(4)
    ]
    for load in loads:
        load.start()
    pl.semaphore_wait(barrier, ROWS - 1 + COLS - 1)

    copies = [
        pltpu.make_async_remote_copy(
            src_ref=sums_ref.at[:, pl.ds(pl.multiple_of(other * 128, 128), 128)],
            dst_ref=shares.at[n],
            send_sem=row_send.at[n],
            recv_sem=row_recv.at[n],
            device_id=(other, col),
            device_id_type=MESH,
        )
        for n, other in enumerate(rows_near)
    ]
    for copy in copies:
        copy.start()
    for copy in copies:
        copy.wait()
    summed = sums_ref[:, pl.ds(pl.multiple_of(row * 128, 128), 128)].astype(F32)
    for n in range(ROWS - 1):
        summed = summed + shares[n].astype(F32)
    reduced[...] = summed.astype(BF16)

    def to_col(n):
        other = lax.rem(col + n, COLS)
        return pltpu.make_async_remote_copy(
            src_ref=reduced.at[pl.ds(pl.multiple_of(other * 16, 16), 16)],
            dst_ref=landed.at[col],
            send_sem=col_send.at[n],
            recv_sem=col_recv.at[n],
            device_id=(row, other),
            device_id_type=MESH,
        )

    def start_col(n, carry):
        to_col(n).start()
        return carry

    lax.fori_loop(1, COLS, start_col, 0)
    landed[col] = reduced[pl.ds(pl.multiple_of(col * 16, 16), 16), :]

    tiles = tile_ref[pl.ds(col, 1), :]
    down = lax.broadcasted_iota(jnp.int32, (128, 128), 0)
    across = lax.broadcasted_iota(jnp.int32, (128, 128), 1)
    spread = jnp.broadcast_to(tiles, (128, 128))
    mine = jnp.sum(jnp.where(down == across, spread, 0), axis=1, keepdims=True)
    earlier = jnp.where((mine == spread) & (across < down), 1, 0)
    rank = jnp.max(earlier, axis=1, keepdims=True)
    tile_col = lax.rem(mine, COLS)
    slot = tile_col // 2 * 16 + (mine // COLS * 2 + lax.rem(tile_col, 2)) * 2 + rank
    select = (
        (slot == lax.broadcasted_iota(jnp.int32, (128, 256), 1)).astype(F32).astype(BF16)
    )

    def wait_col(n, carry):
        to_col(n).wait()
        return carry

    lax.fori_loop(1, COLS, wait_col, 0)
    for load in loads:
        load.wait()
    second = None
    for h in range(2):
        slots = jnp.concatenate([landed[2 * k + h] for k in range(16)], axis=0)
        chosen = jnp.dot(select, slots, preferred_element_type=F32)
        hidden = jnp.maximum(chosen + first_bias_ref[row, h : h + 1, :], 0.0).astype(BF16)
        part = jnp.dot(hidden, second_rows[h], preferred_element_type=F32)
        second = part if second is None else second + part
    parts[...] = second.astype(BF16)
    copies = [
        pltpu.make_async_remote_copy(
            src_ref=parts.at[:, pl.ds(pl.multiple_of(other * 256, 256), 256)],
            dst_ref=final.at[n],
            send_sem=last_send.at[n],
            recv_sem=last_recv.at[n],
            device_id=(other, col),
            device_id_type=MESH,
        )
        for n, other in enumerate(rows_near)
    ]
    for copy in copies:
        copy.start()
    for copy in copies:
        copy.wait()
    summed = parts[:, pl.ds(pl.multiple_of(row * 256, 256), 256)].astype(F32)
    for n in range(ROWS - 1):
        summed = summed + final[n].astype(F32)
    out_ref[...] = jnp.maximum(summed + second_bias_ref[pl.ds(row, 1), :], 0.0).astype(BF16)


def head(sums, tiles, first_bias, second_weight, second_bias):
    return pl.pallas_call(
        head_kernel,
        out_shape=jax.ShapeDtypeStruct((128, 256), BF16),
        in_specs=[VMEM_SPEC, VMEM_SPEC, VMEM_SPEC, pl.BlockSpec(memory_space=pl.ANY), VMEM_SPEC],
        out_specs=VMEM_SPEC,
        scratch_shapes=[
            pltpu.VMEM((ROWS - 1, 512, 128), BF16),
            pltpu.VMEM((512, 128), BF16),
            pltpu.VMEM((COLS, 16, 128), BF16),
            pltpu.VMEM((128, FC), BF16),
            pltpu.VMEM((ROWS - 1, 128, 256), BF16),
            pltpu.VMEM((2, 128, FC), BF16),
            pltpu.SemaphoreType.DMA((ROWS - 1,)),
            pltpu.SemaphoreType.DMA((ROWS - 1,)),
            pltpu.SemaphoreType.DMA((COLS,)),
            pltpu.SemaphoreType.DMA((COLS,)),
            pltpu.SemaphoreType.DMA((ROWS - 1,)),
            pltpu.SemaphoreType.DMA((ROWS - 1,)),
            pltpu.SemaphoreType.DMA((8,)),
        ],
        compiler_params=pltpu.CompilerParams(collective_id=2, has_side_effects=True),
        name="head",
    )(sums, tiles, first_bias, second_weight, second_bias)


def shards(
    tokens,
    project_in,
    project_out,
    expand_weight,
    reduce_weight,
    first_weight,
    first_bias,
    second_weight,
    second_bias,
    box_tile,
    box_shape,
):
    weight = lax.all_gather(
        first_weight.transpose(0, 2, 1),
        "col",
        axis=1,
        tiled=True,
        axis_index_groups=[list(range(core, COLS, 2)) for core in range(2)],
    )
    own, halo = exchange_halo(tokens)
    features, pooled = block(own, halo, project_in, project_out, expand_weight, reduce_weight)
    tiles = box_tile.reshape(COLS, 128)
    codes = (
        (box_shape[:, 0] * 16 + box_shape[:, 1]) * 4
        + (box_shape[:, 2] - 1) * 2
        + (box_shape[:, 3] - 1)
    ).reshape(COLS, 128)
    sums = first_layer(swap_groups(pooled), tiles, codes, weight)
    bias = first_bias.reshape(ROWS, 4, 2, 32).transpose(0, 2, 1, 3).reshape(ROWS, 2, 128)
    box_features = head(sums, tiles, bias, second_weight, second_bias.reshape(ROWS, 256))
    return (features, box_features)


def solution(mesh):
    return jax.shard_map(
        shards,
        mesh=mesh,
        in_specs=(
            P("row", "col", None),
            P(),
            P(),
            P(),
            P(),
            P(None, "row", "col"),
            P(),
            P(),
            P(),
            P(),
            P(),
        ),
        out_specs=(P("row", "col", None), P("col", "row")),
        check_vma=False,
    )
```

```python
import jax
import jax.numpy as jnp
from jax import lax
from jax.experimental import pallas as pl
from jax.experimental.pallas import tpu as pltpu
from jax.sharding import PartitionSpec as P

ROWS = 4
COLS = 32
D = 768
SIDE = 28
HEADS = 12
MLP = 3072
FC = 1024
S0, S1, S2, OWN = 0, 224, 672, 896
TOP, BOT, LEFT, RIGHT, TL, TR, BL, BR, HALO = 0, 256, 512, 736, 960, 1024, 1088, 1152, 1216
HALO_COPIES = (
    (S0 + 160, 64, TOP, 1, 0),
    (S1 + 320, 128, TOP + 64, 1, 0),
    (S2 + 160, 64, TOP + 192, 1, 0),
    (S0, 64, BOT, -1, 0),
    (S1, 128, BOT + 64, -1, 0),
    (S2, 64, BOT + 192, -1, 0),
    (S2, 224, LEFT, 0, 1),
    (S0, 224, RIGHT, 0, -1),
    (S2 + 160, 64, TL, 1, 1),
    (S0 + 160, 64, TR, 1, -1),
    (S2, 64, BL, -1, 1),
    (S0, 64, BR, -1, -1),
)
UNITS = 32
BIN_PARTS = ((0, 13), (13, 12), (25, 12), (37, 12))
GATHER = 28
MESH = pl.DeviceIdType.MESH
F32 = jnp.float32
BF16 = jnp.bfloat16
VMEM_SPEC = pl.BlockSpec(memory_space=pltpu.VMEM)


def norm(values):
    center = values - jnp.mean(values, axis=-1, keepdims=True)
    spread = jnp.mean(center * center, axis=-1, keepdims=True)
    return (center * lax.rsqrt(spread + 1e-6)).astype(BF16)


def window_keys(wy, wx):
    strips = (
        ((False, S0, 8, TOP, BOT), (True, LEFT, 8, TL, BL)),
        ((False, S1, 16, TOP + 64, BOT + 64),),
        ((False, S2, 8, TOP + 192, BOT + 192), (True, RIGHT, 8, TR, BR)),
    )[wx]
    pieces = []
    for outer, base, cells, top, bottom in strips:
        if wy == 0:
            pieces += [(outer, base, 8 * cells), (True, top, 8 * cells)]
        elif wy == 1:
            pieces += [(outer, base + 6 * cells, 16 * cells)]
        else:
            pieces += [(outer, base + 20 * cells, 8 * cells), (True, bottom, 8 * cells)]
    return pieces


def window_bias(wy, wx, row, col):
    lane = lax.broadcasted_iota(jnp.int32, (1, 256), 1)
    cells = 16 if wx == 1 else 8
    line = lax.rem(lane // cells, 16)
    cell = lax.rem(lane, cells)
    if wx == 1:
        keep = cell < 14
    else:
        own_spare, outer_spare = (7, 0) if wx == 0 else (0, 7)
        there = col > 0 if wx == 0 else col < COLS - 1
        keep = ((lane < 128) & (cell != own_spare)) | (
            (lane >= 128) & (cell != outer_spare) & there
        )
    if wy == 0:
        keep = keep & ((line < 7) | ((line > 8) & (row > 0)))
    elif wy == 1:
        keep = keep & (line > 0) & (line < 15)
    else:
        keep = keep & (((line > 0) & (line < 8)) | ((line >= 8) & (line < 15) & (row < ROWS - 1)))
    return jnp.where(keep, 0.0, -1e30).astype(F32)


QUERY_ROWS = [
    ((S0, 56), (S1, 112), (S2, 56)),
    ((S0 + 56, 112), (S1 + 112, 224), (S2 + 56, 112)),
    ((S0 + 168, 56), (S1 + 336, 112), (S2 + 168, 56)),
]


def gather_stages(row, col, part_ref, whole_ref, send_sem, recv_sem):
    z, y, core = col // 8, lax.rem(col // 2, 4), lax.rem(col, 2)
    mine = z * 4 + y
    numbers = iter(range(GATHER))

    def send(to, bins, chunk, width=1, own=False):
        n = next(numbers)
        rows = pl.ds(pl.multiple_of(chunk * UNITS, UNITS), UNITS * width)
        here = whole_ref.at[pl.ds(*bins), rows]
        return pltpu.make_async_remote_copy(
            src_ref=part_ref.at[pl.ds(*bins)] if own else here,
            dst_ref=here,
            send_sem=send_sem.at[n],
            recv_sem=recv_sem.at[n],
            device_id=(row, to),
            device_id_type=MESH,
        )

    def near(dz, dy):
        return lax.rem(z + dz + 4, 4), lax.rem(y + dy + 4, 4)

    def device(dz, dy):
        nz, ny = near(dz, dy)
        return nz * 8 + ny * 2 + core

    first = (0, 25), (25, 24)
    up = [device(0, 1), device(1, 0)]
    down = [device(0, -1), device(-1, 0)]
    steps = ((0, 1), (1, 0))
    stages = [[], [], [], []]
    for axis in range(2):
        for to in (up[axis], down[axis]):
            stages[0].append(send(to, first[axis], mine, own=True))
    for axis in range(2):
        dz, dy = steps[axis]
        for sign, to, part in ((-1, up[axis], 0), (1, down[axis], 1)):
            nz, ny = near(sign * dz, sign * dy)
            stages[1].append(send(to, BIN_PARTS[2 * axis + part], nz * 4 + ny))
    for to in (up[1], down[1]):
        stages[2].append(send(to, first[0], z * 4, 4))
    for to in (up[0], down[0]):
        for n in range(4):
            stages[2].append(send(to, first[1], n * 4 + y))
    for sign, to, part in ((-1, up[1], 0), (1, down[1], 1)):
        stages[3].append(send(to, BIN_PARTS[part], near(sign, 0)[0] * 4, 4))
    for sign, to, part in ((-1, up[0], 2), (1, down[0], 3)):
        for n in range(4):
            stages[3].append(send(to, BIN_PARTS[part], n * 4 + near(0, sign)[1]))
    return stages, [(row, to) for to in up + down], mine


def block_kernel(
    tokens_ref,
    project_in_hbm,
    project_out_hbm,
    expand_hbm,
    reduce_hbm,
    part_ref,
    features_ref,
    pooled_ref,
    whole_ref,
    own_ref,
    halo_ref,
    project_in_ref,
    project_out_ref,
    expand_ref,
    reduce_ref,
    kv_own_ref,
    kv_halo_ref,
    query_ref,
    mixed_ref,
    wide_ref,
    small_ref,
    load_sem,
    send_sem,
    recv_sem,
    gather_send,
    gather_recv,
):
    row, col = lax.axis_index("row"), lax.axis_index("col")
    stages, gather_peers, mine = gather_stages(
        row, col, part_ref, whole_ref, gather_send, gather_recv
    )

    def near(dr, dc):
        return lax.rem(row + dr + ROWS, ROWS), lax.rem(col + dc + COLS, COLS)

    peers = [near(dr, dc) for dr in (-1, 0, 1) for dc in (-1, 0, 1) if (dr, dc) != (0, 0)]
    peers = peers + gather_peers
    barrier = pltpu.get_barrier_semaphore()
    for peer in peers:
        pl.semaphore_signal(barrier, inc=1, device_id=peer, device_id_type=MESH)
    loads = [
        pltpu.make_async_copy(source, target, load_sem.at[n])
        for n, (source, target) in enumerate(
            (
                (project_in_hbm, project_in_ref),
                (project_out_hbm, project_out_ref),
                (expand_hbm, expand_ref),
                (reduce_hbm, reduce_ref),
                (part_ref, whole_ref.at[:, pl.ds(pl.multiple_of(mine * UNITS, UNITS), UNITS)]),
            )
        )
    ]
    for load in loads:
        load.start()
    for y in range(0, SIDE, 2):
        for a in range(2):
            wide_ref[0:6, a, 0:SIDE, :] = jnp.stack(
                [
                    tokens_ref[y + a, :, n * 128 : (n + 1) * 128].astype(F32)
                    for n in range(6)
                ]
            )
        for base, cells, x in ((S0, 8, 0), (S1, 16, 7), (S2, 8, 20)):
            own_ref[base + y * cells : base + (y + 2) * cells, :] = jnp.concatenate(
                [
                    jnp.concatenate(
                        [wide_ref[n, a, x : x + cells, :] for n in range(6)], axis=1
                    )
                    for a in range(2)
                ],
                axis=0,
            ).astype(BF16)
    pl.semaphore_wait(barrier, len(peers))
    halo_copies = [
        pltpu.make_async_remote_copy(
            src_ref=own_ref.at[pl.ds(src, rows)],
            dst_ref=halo_ref.at[pl.ds(dst, rows)],
            send_sem=send_sem.at[n],
            recv_sem=recv_sem.at[n],
            device_id=near(dr, dc),
            device_id_type=MESH,
        )
        for n, (src, rows, dst, dr, dc) in enumerate(HALO_COPIES)
    ]
    for copy in halo_copies:
        copy.start()
    for copy in stages[0]:
        copy.start()

    loads[0].wait()

    def project_own(n, carry):
        at = pl.ds(pl.multiple_of(n * 224, 224), 224)
        normed = norm(own_ref[at, :].astype(F32))
        query_ref[at, :] = (
            jnp.dot(normed, project_in_ref[:, :D], preferred_element_type=F32)
            .astype(BF16)
            .astype(F32)
            * 0.125
        )
        kv_own_ref[at, :] = jnp.dot(
            normed, project_in_ref[:, D:], preferred_element_type=F32
        ).astype(BF16)
        return carry

    lax.fori_loop(0, 4, project_own, 0)
    for copy in halo_copies:
        copy.wait()
    for copy in stages[0]:
        copy.wait_recv()
    for copy in stages[1]:
        copy.start()

    def project_halo(n, carry):
        at = pl.ds(pl.multiple_of(n * 304, 304), 304)
        normed = norm(halo_ref[at, :].astype(F32))
        kv_halo_ref[at, :] = jnp.dot(
            normed, project_in_ref[:, D:], preferred_element_type=F32
        ).astype(BF16)
        return carry

    lax.fori_loop(0, 4, project_halo, 0)
    loads[4].wait()
    for copy in stages[1]:
        copy.wait_recv()
    for copy in stages[2]:
        copy.start()

    left_half = lax.broadcasted_iota(jnp.int32, (1, 128), 1) < 64
    ones = jnp.ones((256, 128), BF16)
    for wy in range(3):
        for wx in range(3):
            start, rows = QUERY_ROWS[wy][wx]
            bias = window_bias(wy, wx, row, col)
            pieces = window_keys(wy, wx)
            for h in range(HEADS // 2):
                lanes = slice(h * 128, (h + 1) * 128)
                asked = query_ref[start : start + rows, lanes]
                both = jnp.concatenate(
                    [jnp.where(left_half, asked, 0.0), jnp.where(left_half, 0.0, asked)],
                    axis=0,
                ).astype(BF16)

                def read(first, pieces=pieces):
                    return jnp.concatenate(
                        [
                            (kv_halo_ref if outer else kv_own_ref)[
                                base : base + count, first : first + 128
                            ]
                            for outer, base, count in pieces
                        ],
                        axis=0,
                    )

                scores = (
                    lax.dot_general(
                        both,
                        read(h * 128),
                        (((1,), (1,)), ((), ())),
                        preferred_element_type=F32,
                    )
                    + bias
                )
                weights = jnp.exp(scores - jnp.max(scores, axis=-1, keepdims=True)).astype(BF16)
                values = jnp.concatenate([read(D + h * 128), ones], axis=1)
                mixed = jnp.dot(weights, values, preferred_element_type=F32)
                mixed = mixed[:, :128] / mixed[:, 128:]
                mixed_ref[start : start + rows, lanes] = jnp.where(
                    left_half, mixed[:rows], mixed[rows:]
                )

    for load in loads[1:4]:
        load.wait()
    for copy in stages[2]:
        copy.wait_recv()
    for copy in stages[3]:
        copy.start()

    def finish(n, carry):
        at = pl.ds(pl.multiple_of(n * 224, 224), 224)
        after = own_ref[at, :].astype(F32) + jnp.dot(
            mixed_ref[at, :].astype(BF16), project_out_ref[...], preferred_element_type=F32
        )
        normed = norm(after)
        total = after
        for part in range(MLP // D):
            units = slice(part * D, (part + 1) * D)
            hidden = jax.nn.gelu(
                jnp.dot(normed, expand_ref[:, units], preferred_element_type=F32)
            ).astype(BF16)
            total = total + jnp.dot(hidden, reduce_ref[units, :], preferred_element_type=F32)
        mixed_ref[at, :] = total.astype(BF16).astype(F32)
        return carry

    lax.fori_loop(0, 4, finish, 0)

    wide_ref[:, :, SIDE:, :] = jnp.zeros((6, SIDE, 32 - SIDE, 128), F32)

    def place_row(y, carry):
        for n in range(6):
            lanes = slice(n * 128, (n + 1) * 128)
            wide_ref[n, y, 0:8, :] = mixed_ref[pl.ds(pl.multiple_of(S0 + y * 8, 8), 8), lanes]
            wide_ref[n, y, 20:28, :] = mixed_ref[pl.ds(pl.multiple_of(S2 + y * 8, 8), 8), lanes]
            middle = mixed_ref[pl.ds(pl.multiple_of(S1 + y * 16, 16), 16), lanes]
            wide_ref[n, y, 7:21, :] = middle[:14]
        features_ref[y] = jnp.concatenate(
            [wide_ref[n, y, 0:SIDE, :] for n in range(6)], axis=1
        ).astype(BF16)
        return carry

    lax.fori_loop(0, SIDE, place_row, 0)

    def pool(u, carry):
        for n in range(6):
            total = (
                wide_ref[n, 2 * u, pl.ds(0, 16, stride=2), :]
                + wide_ref[n, 2 * u, pl.ds(1, 16, stride=2), :]
                + wide_ref[n, 2 * u + 1, pl.ds(0, 16, stride=2), :]
                + wide_ref[n, 2 * u + 1, pl.ds(1, 16, stride=2), :]
            )
            small_ref[pl.ds(pl.multiple_of(u * 16, 16), 16), n * 128 : (n + 1) * 128] = (
                total * 0.25
            )
        return carry

    lax.fori_loop(0, SIDE // 2, pool, 0)
    small_ref[224:256, :] = jnp.zeros((32, D), F32)
    for group, first in enumerate((0, 128, 384, 512)):
        values = small_ref[:, first : first + 256]
        if group % 2:
            values = pltpu.roll(values, 192, 1)
        pooled_ref[group] = values.astype(BF16)


    for copy in stages[3]:
        copy.wait_recv()
    for stage in stages:
        for copy in stage:
            copy.wait_send()


def block(tokens, project_in, project_out, expand_weight, reduce_weight, first_weight):
    bins, units, depth = first_weight.shape
    return pl.pallas_call(
        block_kernel,
        out_shape=(
            jax.ShapeDtypeStruct((SIDE, SIDE, D), BF16),
            jax.ShapeDtypeStruct((ROWS, 256, 256), BF16),
            jax.ShapeDtypeStruct((bins, units * COLS // 2, depth), BF16),
        ),
        in_specs=[VMEM_SPEC] + [pl.BlockSpec(memory_space=pl.ANY)] * 5,
        out_specs=(VMEM_SPEC, VMEM_SPEC, pl.BlockSpec(memory_space=pl.ANY)),
        scratch_shapes=[
            pltpu.VMEM((OWN, D), BF16),
            pltpu.VMEM((HALO, D), BF16),
            pltpu.VMEM((D, 3 * D), BF16),
            pltpu.VMEM((D, D), BF16),
            pltpu.VMEM((D, MLP), BF16),
            pltpu.VMEM((MLP, D), BF16),
            pltpu.VMEM((OWN, 2 * D), BF16),
            pltpu.VMEM((HALO, 2 * D), BF16),
            pltpu.VMEM((OWN, D), F32),
            pltpu.VMEM((OWN, D), F32),
            pltpu.VMEM((6, SIDE, 32, 128), F32),
            pltpu.VMEM((256, D), F32),
            pltpu.SemaphoreType.DMA((5,)),
            pltpu.SemaphoreType.DMA((len(HALO_COPIES),)),
            pltpu.SemaphoreType.DMA((len(HALO_COPIES),)),
            pltpu.SemaphoreType.DMA((GATHER,)),
            pltpu.SemaphoreType.DMA((GATHER,)),
        ],
        compiler_params=pltpu.CompilerParams(
            collective_id=0, has_side_effects=True, vmem_limit_bytes=60 * 1024 * 1024
        ),
        cost_estimate=pl.CostEstimate(
            flops=18_000_000_000, bytes_accessed=22_000_000, transcendentals=6_000_000
        ),
        name="block",
    )(tokens, project_in, project_out, expand_weight, reduce_weight, first_weight)


def boxes_kernel(
    pooled_ref,
    tile_ref,
    code_ref,
    weight_hbm,
    first_bias_ref,
    second_hbm,
    second_bias_ref,
    out_ref,
    group_ref,
    weight_ref,
    code_at,
    crops,
    total,
    sums_ref,
    shares,
    reduced,
    landed,
    parts,
    final,
    second_rows,
    own_sem,
    weight_sem,
    second_sem,
    swap_send,
    swap_recv,
    row_send,
    row_recv,
    col_send,
    col_recv,
    last_send,
    last_recv,
):
    row, col = lax.axis_index("row"), lax.axis_index("col")
    base, core = col // 2 * 2, lax.rem(col, 2)
    rows_near = [lax.rem(row + n, ROWS) for n in range(1, ROWS)]
    barrier = pltpu.get_barrier_semaphore()
    for other in rows_near:
        for side in range(2):
            pl.semaphore_signal(
                barrier, inc=1, device_id=(other, base + side), device_id_type=MESH
            )

    def greet_col(n, carry):
        pl.semaphore_signal(
            barrier, inc=1, device_id=(row, lax.rem(col + n, COLS)), device_id_type=MESH
        )
        return carry

    lax.fori_loop(1, COLS, greet_col, 0)
    me = row * 2 + core
    own = pltpu.make_async_copy(pooled_ref.at[row], group_ref.at[me], own_sem)
    own.start()
    weight_loads = [
        pltpu.make_async_copy(
            weight_hbm.at[pl.ds(i * 7, 7)], weight_ref.at[pl.ds(i * 7, 7)], weight_sem.at[i]
        )
        for i in range(7)
    ]
    for load in weight_loads:
        load.start()
    second_loads = [
        pltpu.make_async_copy(
            second_hbm.at[pl.ds(row * 256 + k * 64 + h * 32, 32)],
            second_rows.at[h, pl.ds(k * 32, 32)],
            second_sem.at[h * 4 + k],
        )
        for h in range(2)
        for k in range(4)
    ]
    for load in second_loads:
        load.start()
    pl.semaphore_wait(barrier, 2 * (ROWS - 1) + COLS - 1)

    others = [lax.rem(me + n, 8) for n in range(1, 8)]
    swaps = [
        pltpu.make_async_remote_copy(
            src_ref=pooled_ref.at[other // 2],
            dst_ref=group_ref.at[me],
            send_sem=swap_send.at[n],
            recv_sem=swap_recv.at[n],
            device_id=(other // 2, base + lax.rem(other, 2)),
            device_id_type=MESH,
        )
        for n, other in enumerate(others)
    ]
    for copy in swaps:
        copy.start()

    lane = lax.broadcasted_iota(jnp.int32, (COLS, 128), 1)
    for t in range(8):
        here = tile_ref[...] == t // 2 * COLS + base + t % 2
        first = jnp.min(jnp.where(here, lane, 127), axis=1, keepdims=True)
        last = jnp.max(jnp.where(here, lane, 0), axis=1, keepdims=True)
        for rank, pick in enumerate((first, last)):
            code = jnp.sum(jnp.where(lane == pick, code_ref[...], 0), axis=1, keepdims=True)
            code_at[t, rank * COLS : (rank + 1) * COLS, :] = jnp.broadcast_to(code, (COLS, 128))
    total[...] = jnp.zeros_like(total)

    tiles = tile_ref[pl.ds(col, 1), :]
    down = lax.broadcasted_iota(jnp.int32, (128, 128), 0)
    across = lax.broadcasted_iota(jnp.int32, (128, 128), 1)
    spread = jnp.broadcast_to(tiles, (128, 128))
    mine = jnp.sum(jnp.where(down == across, spread, 0), axis=1, keepdims=True)
    earlier = jnp.where((mine == spread) & (across < down), 1, 0)
    rank = jnp.max(earlier, axis=1, keepdims=True)
    tile_col = lax.rem(mine, COLS)
    slot = tile_col // 2 * 16 + (mine // COLS * 2 + lax.rem(tile_col, 2)) * 2 + rank
    select = (
        (slot == lax.broadcasted_iota(jnp.int32, (128, 256), 1)).astype(F32).astype(BF16)
    )
    to = lax.broadcasted_iota(jnp.int32, (512, 512), 0)
    source = lax.rem(to // 2, 8) * 64 + lax.rem(to, 2) * 32 + to // 16
    order = (source == lax.broadcasted_iota(jnp.int32, (512, 512), 1)).astype(F32).astype(BF16)

    own.wait()
    for copy in swaps:
        copy.wait()
    spot = lax.broadcasted_iota(jnp.int32, (64, 128), 1)

    def bin_row(i, carry):
        load = pltpu.make_async_copy(
            weight_hbm.at[pl.ds(i * 7, 7)], weight_ref.at[pl.ds(i * 7, 7)], weight_sem.at[i]
        )
        for t in range(8):
            code = code_at[t]
            below = 1 + lax.rem(code // 2, 2)
            right = 1 + lax.rem(code, 2)
            position = code // 4 + i * 16 * below
            picks = []
            for j in range(7):
                low = (position == spot).astype(F32)
                high = (position == spot + 128).astype(F32)
                picks.append(jnp.concatenate([low, high], axis=1).astype(BF16))
                position = position + right
            found = jnp.dot(
                jnp.concatenate(picks, axis=0), group_ref[t], preferred_element_type=F32
            ).astype(BF16)
            for j in range(7):
                crops[j, t * 64 : (t + 1) * 64, :] = found[j * 64 : (j + 1) * 64, :192]
        load.wait()
        summed = total[...]
        for j in range(7):
            summed = summed + lax.dot_general(
                crops[j],
                weight_ref[i * 7 + j],
                (((1,), (1,)), ((), ())),
                preferred_element_type=F32,
            )
        total[...] = summed
        return carry

    lax.fori_loop(0, 7, bin_row, 0)
    sums_ref[...] = jnp.dot(
        order, total[...].astype(BF16), preferred_element_type=F32
    ).astype(BF16)

    copies = [
        pltpu.make_async_remote_copy(
            src_ref=sums_ref.at[:, pl.ds(pl.multiple_of(other * 128, 128), 128)],
            dst_ref=shares.at[n],
            send_sem=row_send.at[n],
            recv_sem=row_recv.at[n],
            device_id=(other, col),
            device_id_type=MESH,
        )
        for n, other in enumerate(rows_near)
    ]
    for copy in copies:
        copy.start()
    for copy in copies:
        copy.wait()
    summed = sums_ref[:, pl.ds(pl.multiple_of(row * 128, 128), 128)].astype(F32)
    for n in range(ROWS - 1):
        summed = summed + shares[n].astype(F32)
    reduced[...] = summed.astype(BF16)

    def to_col(n):
        other = lax.rem(col + n, COLS)
        return pltpu.make_async_remote_copy(
            src_ref=reduced.at[pl.ds(pl.multiple_of(other * 16, 16), 16)],
            dst_ref=landed.at[col],
            send_sem=col_send.at[n],
            recv_sem=col_recv.at[n],
            device_id=(row, other),
            device_id_type=MESH,
        )

    def start_col(n, carry):
        to_col(n).start()
        return carry

    lax.fori_loop(1, COLS, start_col, 0)
    landed[col] = reduced[pl.ds(pl.multiple_of(col * 16, 16), 16), :]

    def wait_col(n, carry):
        to_col(n).wait()
        return carry

    lax.fori_loop(1, COLS, wait_col, 0)
    for load in second_loads:
        load.wait()
    second = None
    for h in range(2):
        slots = jnp.concatenate([landed[2 * k + h] for k in range(16)], axis=0)
        chosen = jnp.dot(select, slots, preferred_element_type=F32)
        hidden = jnp.maximum(chosen + first_bias_ref[row, h : h + 1, :], 0.0).astype(BF16)
        part = jnp.dot(hidden, second_rows[h], preferred_element_type=F32)
        second = part if second is None else second + part
    parts[...] = second.astype(BF16)
    copies = [
        pltpu.make_async_remote_copy(
            src_ref=parts.at[:, pl.ds(pl.multiple_of(other * 256, 256), 256)],
            dst_ref=final.at[n],
            send_sem=last_send.at[n],
            recv_sem=last_recv.at[n],
            device_id=(other, col),
            device_id_type=MESH,
        )
        for n, other in enumerate(rows_near)
    ]
    for copy in copies:
        copy.start()
    for copy in copies:
        copy.wait()
    summed = parts[:, pl.ds(pl.multiple_of(row * 256, 256), 256)].astype(F32)
    for n in range(ROWS - 1):
        summed = summed + final[n].astype(F32)
    out_ref[...] = jnp.maximum(summed + second_bias_ref[pl.ds(row, 1), :], 0.0).astype(BF16)


def boxes(pooled, tiles, codes, weight, first_bias, second_weight, second_bias):
    bins, units, depth = weight.shape
    dma = pltpu.SemaphoreType.DMA
    return pl.pallas_call(
        boxes_kernel,
        out_shape=jax.ShapeDtypeStruct((128, 256), BF16),
        in_specs=[
            VMEM_SPEC,
            VMEM_SPEC,
            VMEM_SPEC,
            pl.BlockSpec(memory_space=pl.ANY),
            VMEM_SPEC,
            pl.BlockSpec(memory_space=pl.ANY),
            VMEM_SPEC,
        ],
        out_specs=VMEM_SPEC,
        scratch_shapes=[
            pltpu.VMEM((8, 256, 256), BF16),
            pltpu.VMEM((bins, units, depth), BF16),
            pltpu.VMEM((8, 64, 128), jnp.int32),
            pltpu.VMEM((7, units, depth), BF16),
            pltpu.VMEM((512, units), F32),
            pltpu.VMEM((512, units), BF16),
            pltpu.VMEM((ROWS - 1, 512, 128), BF16),
            pltpu.VMEM((512, 128), BF16),
            pltpu.VMEM((COLS, 16, 128), BF16),
            pltpu.VMEM((128, FC), BF16),
            pltpu.VMEM((ROWS - 1, 128, 256), BF16),
            pltpu.VMEM((2, 128, FC), BF16),
            dma,
            dma((7,)),
            dma((8,)),
            dma((7,)),
            dma((7,)),
            dma((ROWS - 1,)),
            dma((ROWS - 1,)),
            dma((COLS,)),
            dma((COLS,)),
            dma((ROWS - 1,)),
            dma((ROWS - 1,)),
        ],
        compiler_params=pltpu.CompilerParams(
            collective_id=1, has_side_effects=True, vmem_limit_bytes=56 * 1024 * 1024
        ),
        cost_estimate=pl.CostEstimate(
            flops=9_000_000_000, bytes_accessed=12_000_000, transcendentals=0
        ),
        name="boxes",
    )(pooled, tiles, codes, weight, first_bias, second_weight, second_bias)


def shards(
    tokens,
    project_in,
    project_out,
    expand_weight,
    reduce_weight,
    first_weight,
    first_bias,
    second_weight,
    second_bias,
    box_tile,
    box_shape,
):
    features, pooled, weight = block(
        tokens,
        project_in,
        project_out,
        expand_weight,
        reduce_weight,
        first_weight.transpose(0, 2, 1),
    )
    tiles = box_tile.reshape(COLS, 128)
    codes = (
        (box_shape[:, 0] * 16 + box_shape[:, 1]) * 4
        + (box_shape[:, 2] - 1) * 2
        + (box_shape[:, 3] - 1)
    ).reshape(COLS, 128)
    bias = first_bias.reshape(ROWS, 4, 2, 32).transpose(0, 2, 1, 3).reshape(ROWS, 2, 128)
    box_features = boxes(
        pooled, tiles, codes, weight, bias, second_weight, second_bias.reshape(ROWS, 256)
    )
    return (features, box_features)


def solution(mesh):
    return jax.shard_map(
        shards,
        mesh=mesh,
        in_specs=(
            P("row", "col", None),
            P(),
            P(),
            P(),
            P(),
            P(None, "row", "col"),
            P(),
            P(),
            P(),
            P(),
            P(),
        ),
        out_specs=(P("row", "col", None), P("col", "row")),
        check_vma=False,
    )
```

```python
import jax
import jax.numpy as jnp
from jax import lax
from jax.experimental import pallas as pl
from jax.experimental.pallas import tpu as pltpu
from jax.sharding import PartitionSpec as P

ROWS = 4
COLS = 32
D = 768
SIDE = 28
HEADS = 12
MLP = 3072
FC = 1024
S0, S1, S2, OWN = 0, 224, 672, 896
TOP, BOT, LEFT, RIGHT, TL, TR, BL, BR, HALO = 0, 256, 512, 736, 960, 1024, 1088, 1152, 1216
HALO_COPIES = (
    (S0 + 160, 64, TOP, 1, 0),
    (S1 + 320, 128, TOP + 64, 1, 0),
    (S2 + 160, 64, TOP + 192, 1, 0),
    (S0, 64, BOT, -1, 0),
    (S1, 128, BOT + 64, -1, 0),
    (S2, 64, BOT + 192, -1, 0),
    (S2, 224, LEFT, 0, 1),
    (S0, 224, RIGHT, 0, -1),
    (S2 + 160, 64, TL, 1, 1),
    (S0 + 160, 64, TR, 1, -1),
    (S2, 64, BL, -1, 1),
    (S0, 64, BR, -1, -1),
)
QUADS = 12
TILES = 6 * QUADS + 2
HALVES = ((0, 36), (36, 38))
QUARTERS = ((0, 18), (18, 18), (36, 18), (54, 20))
GATHER = 25
UNITS = 32
MESH = pl.DeviceIdType.MESH
F32 = jnp.float32
BF16 = jnp.bfloat16
VMEM_SPEC = pl.BlockSpec(memory_space=pltpu.VMEM)


def norm(values):
    center = values - jnp.mean(values, axis=-1, keepdims=True)
    spread = jnp.mean(center * center, axis=-1, keepdims=True)
    return (center * lax.rsqrt(spread + 1e-6)).astype(BF16)


def window_keys(wy, wx):
    strips = (
        ((False, S0, 8, TOP, BOT), (True, LEFT, 8, TL, BL)),
        ((False, S1, 16, TOP + 64, BOT + 64),),
        ((False, S2, 8, TOP + 192, BOT + 192), (True, RIGHT, 8, TR, BR)),
    )[wx]
    pieces = []
    for outer, base, cells, top, bottom in strips:
        if wy == 0:
            pieces += [(outer, base, 8 * cells), (True, top, 8 * cells)]
        elif wy == 1:
            pieces += [(outer, base + 6 * cells, 16 * cells)]
        else:
            pieces += [(outer, base + 20 * cells, 8 * cells), (True, bottom, 8 * cells)]
    return pieces


def window_bias(wy, wx, row, col):
    lane = lax.broadcasted_iota(jnp.int32, (1, 256), 1)
    cells = 16 if wx == 1 else 8
    line = lax.rem(lane // cells, 16)
    cell = lax.rem(lane, cells)
    if wx == 1:
        keep = cell < 14
    else:
        own_spare, outer_spare = (7, 0) if wx == 0 else (0, 7)
        there = col > 0 if wx == 0 else col < COLS - 1
        keep = ((lane < 128) & (cell != own_spare)) | (
            (lane >= 128) & (cell != outer_spare) & there
        )
    if wy == 0:
        keep = keep & ((line < 7) | ((line > 8) & (row > 0)))
    elif wy == 1:
        keep = keep & (line > 0) & (line < 15)
    else:
        keep = keep & (((line > 0) & (line < 8)) | ((line >= 8) & (line < 15) & (row < ROWS - 1)))
    return jnp.where(keep, 0.0, -1e30).astype(F32)


QUERY_ROWS = [
    ((S0, 56), (S1, 112), (S2, 56)),
    ((S0 + 56, 112), (S1 + 112, 224), (S2 + 56, 112)),
    ((S0 + 168, 56), (S1 + 336, 112), (S2 + 168, 56)),
]


def gather_stages(row, col, whole_ref, send_sem, recv_sem):
    z, y, core = col // 8, lax.rem(col // 2, 4), lax.rem(col, 2)
    numbers = iter(range(GATHER))

    def send(to, place):
        n = next(numbers)
        return pltpu.make_async_remote_copy(
            src_ref=whole_ref.at[place],
            dst_ref=whole_ref.at[place],
            send_sem=send_sem.at[n],
            recv_sem=recv_sem.at[n],
            device_id=(row, to),
            device_id_type=MESH,
        )

    def device(dz, dy):
        return lax.rem(z + dz + 4, 4) * 8 + lax.rem(y + dy + 4, 4) * 2 + core

    def step(at, by):
        return lax.rem(at + by + 4, 4)

    up = [device(0, 1), device(1, 0)]
    down = [device(0, -1), device(-1, 0)]
    stages = [[], [], [], []]
    for axis in range(2):
        for to in (up[axis], down[axis]):
            stages[0].append(send(to, (z, y, pl.ds(*HALVES[axis]))))
    for axis in range(2):
        for sign, to, part in ((-1, up[axis], 0), (1, down[axis], 1)):
            chunk = (z, step(y, sign)) if axis == 0 else (step(z, sign), y)
            stages[1].append(send(to, (*chunk, pl.ds(*QUARTERS[2 * axis + part]))))
    for to in (up[1], down[1]):
        stages[2].append(send(to, (z, slice(None), pl.ds(*HALVES[0]))))
    for to in (up[0], down[0]):
        stages[2].append(send(to, (slice(None), y, pl.ds(*HALVES[1]))))
    for n in range(3):
        for quarter in range(4):
            sign, to = ((-1, up), (1, down))[quarter % 2]
            tiles = pl.ds(QUARTERS[quarter][0] + 6 * n, 6)
            if quarter < 2:
                place = (step(z, sign), slice(None), tiles)
            else:
                place = (slice(None), step(y, sign), tiles)
            stages[3].append(send(to[1 - quarter // 2], place))
    stages[3].append(send(down[0], (slice(None), step(y, 1), pl.ds(6 * QUADS, 2))))
    return stages


def whole_kernel(
    tokens_ref,
    project_in_hbm,
    project_out_hbm,
    expand_hbm,
    reduce_hbm,
    part_hbm,
    tile_ref,
    code_ref,
    first_bias_ref,
    second_hbm,
    second_bias_ref,
    features_hbm,
    out_ref,
    own_ref,
    halo_ref,
    project_in_ref,
    project_out_ref,
    expand_ref,
    reduce_ref,
    kv_own_ref,
    kv_halo_ref,
    query_ref,
    mixed_ref,
    wide_ref,
    small_ref,
    features_ref,
    part_ref,
    whole_ref,
    pooled_ref,
    packed_ref,
    group_ref,
    code_at,
    crops,
    sums_ref,
    ahead_ref,
    passed,
    shares,
    reduced,
    landed,
    parts,
    final,
    second_rows,
    load_sem,
    halo_send,
    halo_recv,
    gather_send,
    gather_recv,
    features_sem,
    swap_send,
    swap_recv,
    pair_send,
    pair_recv,
    row_send,
    row_recv,
    col_send,
    col_recv,
    last_send,
    last_recv,
):
    row, col = lax.axis_index("row"), lax.axis_index("col")
    core = lax.rem(col, 2)
    rows_near = [lax.rem(row + n, ROWS) for n in range(1, ROWS)]
    base = col - core
    stages = gather_stages(row, col, whole_ref, gather_send, gather_recv)

    def remote(source, target, send, recv, to):
        return pltpu.make_async_remote_copy(
            src_ref=source,
            dst_ref=target,
            send_sem=send,
            recv_sem=recv,
            device_id=to,
            device_id_type=MESH,
        )

    def near(dr, dc):
        return lax.rem(row + dr + ROWS, ROWS), lax.rem(col + dc + COLS, COLS)

    barrier = pltpu.get_barrier_semaphore()
    greeted = [near(dr, dc) for dr in (-1, 1) for dc in (-1, 0, 1)] + [near(2, 0)]
    for peer in greeted:
        pl.semaphore_signal(barrier, inc=1, device_id=peer, device_id_type=MESH)

    def greet_col(n, carry):
        pl.semaphore_signal(barrier, inc=1, device_id=near(0, n), device_id_type=MESH)
        return carry

    lax.fori_loop(1, COLS, greet_col, 0)
    loads = [
        pltpu.make_async_copy(source, target, load_sem.at[n])
        for n, (source, target) in enumerate(
            [
                (part_hbm, part_ref),
                (project_in_hbm, project_in_ref),
                (project_out_hbm, project_out_ref),
                (expand_hbm, expand_ref),
                (reduce_hbm, reduce_ref),
            ]
            + [
                (
                    second_hbm.at[pl.ds(row * 256 + k * 64 + h * 32, 32)],
                    second_rows.at[h, pl.ds(k * 32, 32)],
                )
                for h in range(2)
                for k in range(4)
            ]
        )
    ]
    for load in loads:
        load.start()
    for y in range(0, SIDE, 2):
        for a in range(2):
            wide_ref[0:6, a, 0:SIDE, :] = jnp.stack(
                [
                    tokens_ref[y + a, :, n * 128 : (n + 1) * 128].astype(F32)
                    for n in range(6)
                ]
            )
        for strip, cells, x in ((S0, 8, 0), (S1, 16, 7), (S2, 8, 20)):
            own_ref[strip + y * cells : strip + (y + 2) * cells, :] = jnp.concatenate(
                [
                    jnp.concatenate(
                        [wide_ref[n, a, x : x + cells, :] for n in range(6)], axis=1
                    )
                    for a in range(2)
                ],
                axis=0,
            ).astype(BF16)
    pl.semaphore_wait(barrier, len(greeted) + COLS - 1)
    halo_copies = [
        remote(
            own_ref.at[pl.ds(src, rows)],
            halo_ref.at[pl.ds(dst, rows)],
            halo_send.at[n],
            halo_recv.at[n],
            near(dr, dc),
        )
        for n, (src, rows, dst, dr, dc) in enumerate(HALO_COPIES)
    ]
    for copy in halo_copies:
        copy.start()

    z, y = col // 8, lax.rem(col // 2, 4)
    loads[0].wait()

    def pack(q, carry):
        four = [part_ref[4 * q + m].astype(F32) for m in range(4)]
        for m in range(4):
            whole_ref[z, y, 6 * q + m] = four[m][:, :128].astype(BF16)
        for m in range(2):
            whole_ref[z, y, 6 * q + 4 + m] = jnp.concatenate(
                [four[2 * m][:, 128:], four[2 * m + 1][:, 128:]], axis=1
            ).astype(BF16)
        return carry

    lax.fori_loop(0, QUADS, pack, 0)
    last = part_ref[4 * QUADS].astype(F32)
    whole_ref[z, y, 6 * QUADS] = last[:, :128].astype(BF16)
    whole_ref[z, y, 6 * QUADS + 1] = jnp.concatenate(
        [last[:, 128:], jnp.zeros((UNITS, 64), F32)], axis=1
    ).astype(BF16)
    for copy in stages[0]:
        copy.start()

    loads[1].wait()

    def project_own(n, carry):
        at = pl.ds(pl.multiple_of(n * 224, 224), 224)
        normed = norm(own_ref[at, :].astype(F32))
        query_ref[at, :] = (
            jnp.dot(normed, project_in_ref[:, :D], preferred_element_type=F32)
            .astype(BF16)
            .astype(F32)
            * 0.125
        )
        kv_own_ref[at, :] = jnp.dot(
            normed, project_in_ref[:, D:], preferred_element_type=F32
        ).astype(BF16)
        return carry

    lax.fori_loop(0, 4, project_own, 0)
    for copy in halo_copies:
        copy.wait()

    def project_halo(n, carry):
        at = pl.ds(pl.multiple_of(n * 304, 304), 304)
        normed = norm(halo_ref[at, :].astype(F32))
        kv_halo_ref[at, :] = jnp.dot(
            normed, project_in_ref[:, D:], preferred_element_type=F32
        ).astype(BF16)
        return carry

    lax.fori_loop(0, 4, project_halo, 0)
    for copy in stages[0]:
        copy.wait_recv()
    for copy in stages[1]:
        copy.start()

    left_half = lax.broadcasted_iota(jnp.int32, (1, 128), 1) < 64
    ones = jnp.ones((256, 128), BF16)
    for wy in range(3):
        if wy == 1:
            for copy in stages[1]:
                copy.wait_recv()
            for copy in stages[2]:
                copy.start()
        for wx in range(3):
            start, rows = QUERY_ROWS[wy][wx]
            bias = window_bias(wy, wx, row, col)
            pieces = window_keys(wy, wx)
            for h in range(HEADS // 2):
                lanes = slice(h * 128, (h + 1) * 128)
                asked = query_ref[start : start + rows, lanes]
                both = jnp.concatenate(
                    [jnp.where(left_half, asked, 0.0), jnp.where(left_half, 0.0, asked)],
                    axis=0,
                ).astype(BF16)

                def read(first, pieces=pieces):
                    return jnp.concatenate(
                        [
                            (kv_halo_ref if outer else kv_own_ref)[
                                place : place + count, first : first + 128
                            ]
                            for outer, place, count in pieces
                        ],
                        axis=0,
                    )

                scores = (
                    lax.dot_general(
                        both,
                        read(h * 128),
                        (((1,), (1,)), ((), ())),
                        preferred_element_type=F32,
                    )
                    + bias
                )
                weights = jnp.exp(scores - jnp.max(scores, axis=-1, keepdims=True)).astype(BF16)
                values = jnp.concatenate([read(D + h * 128), ones], axis=1)
                mixed = jnp.dot(weights, values, preferred_element_type=F32)
                mixed = mixed[:, :128] / mixed[:, 128:]
                mixed_ref[start : start + rows, lanes] = jnp.where(
                    left_half, mixed[:rows], mixed[rows:]
                )

    for load in loads[2:]:
        load.wait()

    def finish(n, carry):
        at = pl.ds(pl.multiple_of(n * 224, 224), 224)
        after = own_ref[at, :].astype(F32) + jnp.dot(
            mixed_ref[at, :].astype(BF16), project_out_ref[...], preferred_element_type=F32
        )
        normed = norm(after)
        total = after
        for part in range(MLP // D):
            units = slice(part * D, (part + 1) * D)
            hidden = jax.nn.gelu(
                jnp.dot(normed, expand_ref[:, units], preferred_element_type=F32)
            ).astype(BF16)
            total = total + jnp.dot(hidden, reduce_ref[units, :], preferred_element_type=F32)
        mixed_ref[at, :] = total.astype(BF16).astype(F32)
        return carry

    lax.fori_loop(0, 4, finish, 0)

    wide_ref[:, :, SIDE:, :] = jnp.zeros((6, SIDE, 32 - SIDE, 128), F32)

    def place_row(y, carry):
        for n in range(6):
            lanes = slice(n * 128, (n + 1) * 128)
            wide_ref[n, y, 0:8, :] = mixed_ref[pl.ds(pl.multiple_of(S0 + y * 8, 8), 8), lanes]
            wide_ref[n, y, 20:28, :] = mixed_ref[pl.ds(pl.multiple_of(S2 + y * 8, 8), 8), lanes]
            middle = mixed_ref[pl.ds(pl.multiple_of(S1 + y * 16, 16), 16), lanes]
            wide_ref[n, y, 7:21, :] = middle[:14]
        features_ref[y] = jnp.concatenate(
            [wide_ref[n, y, 0:SIDE, :] for n in range(6)], axis=1
        ).astype(BF16)
        return carry

    lax.fori_loop(0, SIDE, place_row, 0)

    def pool(u, carry):
        for n in range(6):
            total = (
                wide_ref[n, 2 * u, pl.ds(0, 16, stride=2), :]
                + wide_ref[n, 2 * u, pl.ds(1, 16, stride=2), :]
                + wide_ref[n, 2 * u + 1, pl.ds(0, 16, stride=2), :]
                + wide_ref[n, 2 * u + 1, pl.ds(1, 16, stride=2), :]
            )
            small_ref[pl.ds(pl.multiple_of(u * 16, 16), 16), n * 128 : (n + 1) * 128] = (
                total * 0.25
            )
        return carry

    lax.fori_loop(0, SIDE // 2, pool, 0)
    features_out = pltpu.make_async_copy(features_ref, features_hbm, features_sem)
    features_out.start()
    near_half = lax.broadcasted_iota(jnp.int32, (112, 128), 1) < 64
    for group, first in enumerate((0, 128, 384, 512)):
        values = small_ref[:, first : first + 256]
        if group % 2:
            values = pltpu.roll(values, 192, 1)
        rest = jnp.where(
            near_half, values[:112, 128:], pltpu.roll(values[112:, 128:], 64, 1)
        )
        pooled_ref[group] = jnp.concatenate(
            [values[:112, :128], values[112:, :128], rest], axis=1
        ).astype(BF16)

    swaps = []
    for n in range(1, ROWS):
        other = lax.rem(row + n, ROWS)
        swaps.append(
            remote(
                pooled_ref.at[other],
                packed_ref.at[core, row],
                swap_send.at[n - 1],
                swap_recv.at[n - 1],
                (other, col),
            )
        )
    for copy in swaps:
        copy.start()
    packed_ref[core, row] = pooled_ref[row]

    def to_pair(n):
        there = lax.rem(row - n + ROWS, ROWS)
        return remote(
            packed_ref.at[core, there],
            packed_ref.at[core, there],
            pair_send.at[n],
            pair_recv.at[n],
            (row, base + 1 - core),
        )

    pairs = [to_pair(n) for n in range(ROWS)]
    pairs[0].start()

    lane = lax.broadcasted_iota(jnp.int32, (COLS, 128), 1)
    for t in range(8):
        here = tile_ref[...] == t // 2 * COLS + base + t % 2
        first = jnp.min(jnp.where(here, lane, 127), axis=1, keepdims=True)
        last = jnp.max(jnp.where(here, lane, 0), axis=1, keepdims=True)
        for rank, pick in enumerate((first, last)):
            code = jnp.sum(jnp.where(lane == pick, code_ref[...], 0), axis=1, keepdims=True)
            code_at[t, rank * COLS : (rank + 1) * COLS, :] = jnp.broadcast_to(code, (COLS, 128))

    tiles = tile_ref[pl.ds(col, 1), :]
    down = lax.broadcasted_iota(jnp.int32, (128, 128), 0)
    across = lax.broadcasted_iota(jnp.int32, (128, 128), 1)
    spread = jnp.broadcast_to(tiles, (128, 128))
    mine = jnp.sum(jnp.where(down == across, spread, 0), axis=1, keepdims=True)
    earlier = jnp.where((mine == spread) & (across < down), 1, 0)
    rank = jnp.max(earlier, axis=1, keepdims=True)
    tile_col = lax.rem(mine, COLS)
    slot = tile_col // 2 * 16 + (mine // COLS * 2 + lax.rem(tile_col, 2)) * 2 + rank
    select = (
        (slot == lax.broadcasted_iota(jnp.int32, (128, 256), 1)).astype(F32).astype(BF16)
    )
    to = lax.broadcasted_iota(jnp.int32, (512, 512), 0)
    source = lax.rem(to // 2, 8) * 64 + lax.rem(to, 2) * 32 + to // 16
    order = (source == lax.broadcasted_iota(jnp.int32, (512, 512), 1)).astype(F32).astype(BF16)

    for n in range(1, ROWS):
        swaps[n - 1].wait_recv()
        pairs[n].start()
    for copy in stages[2]:
        copy.wait_recv()
    for copy in stages[3]:
        copy.start()
    for copy in pairs:
        copy.wait_recv()

    group_ref[:, 224:, :] = jnp.zeros((8, 32, 256), BF16)
    for t in range(8):
        packed = packed_ref[t % 2, t // 2].astype(F32)
        rest = packed[:, 256:]
        turned = pltpu.roll(rest, 64, 1)
        group_ref[t, 0:112, :] = jnp.concatenate(
            [packed[:, :128], jnp.where(near_half, rest, turned)], axis=1
        ).astype(BF16)
        group_ref[t, 112:224, :] = jnp.concatenate(
            [packed[:, 128:256], jnp.where(near_half, turned, rest)], axis=1
        ).astype(BF16)

    spot = lax.broadcasted_iota(jnp.int32, (64, 128), 1)
    near_lanes = spot < 64

    def sample(t, bins):
        code = code_at[t]
        below = 16 * (1 + lax.rem(code // 2, 2))
        right = 1 + lax.rem(code, 2)
        picks = []
        for bin in bins:
            position = code // 4 + (bin // 7) * below + (bin % 7) * right
            low = (position == spot).astype(F32)
            high = (position == spot + 128).astype(F32)
            picks.append(jnp.concatenate([low, high], axis=1).astype(BF16))
        return jnp.dot(
            jnp.concatenate(picks, axis=0), group_ref[t], preferred_element_type=F32
        )

    def multiply(width, tile):
        weight = jnp.concatenate(
            [whole_ref[:, :, tile + n].reshape(16 * UNITS, 128) for n in range(width)], axis=1
        )
        return lax.dot_general(
            crops[:, : 128 * width],
            weight,
            (((1,), (1,)), ((), ())),
            preferred_element_type=F32,
        )

    stages[3][12].wait_recv()
    for t in range(8):
        crops[t * 64 : (t + 1) * 64, :256] = sample(t, (4 * QUADS,)).astype(BF16)
    total = mixed_ref.at[0:512, 0:512]
    total[...] = multiply(2, 6 * QUADS)
    for n in range(3):
        for quarter in range(4):
            quad = 3 * quarter + n
            for t in range(8):
                found = sample(t, range(4 * quad, 4 * quad + 4))
                for m in range(4):
                    crops[t * 64 : (t + 1) * 64, m * 128 : (m + 1) * 128] = found[
                        m * 64 : (m + 1) * 64, :128
                    ].astype(BF16)
                for m in range(2):
                    crops[t * 64 : (t + 1) * 64, (4 + m) * 128 : (5 + m) * 128] = jnp.where(
                        near_lanes,
                        found[m * 128 : m * 128 + 64, 128:],
                        found[m * 128 + 64 : m * 128 + 128, 128:],
                    ).astype(BF16)
            stages[3][4 * n + quarter].wait_recv()
            total[...] += multiply(6, 6 * quad)
    sums_ref[...] = jnp.dot(
        order, total[...].astype(BF16), preferred_element_type=F32
    ).astype(BF16)

    def share(n):
        return pl.ds(pl.multiple_of(lax.rem(row + n + ROWS, ROWS) * 128, 128), 128)

    sides = ((1, 0), (-1, 256))
    far = [
        remote(
            sums_ref.at[pl.ds(first, 256), share(2)],
            passed.at[n],
            row_send.at[n],
            row_recv.at[n],
            near(dr, 0),
        )
        for n, (dr, first) in enumerate(sides)
    ]
    for copy in far:
        copy.start()
    for copy in far:
        copy.wait_recv()
    close = []
    for n, (dr, first) in enumerate(sides):
        ahead_ref[n] = sums_ref[:, share(dr)]
        ahead_ref[n, first : first + 256, :] = (
            sums_ref[first : first + 256, share(dr)].astype(F32) + passed[n].astype(F32)
        ).astype(BF16)
        close.append(
            remote(ahead_ref.at[n], shares.at[n], row_send.at[2 + n], row_recv.at[2 + n], near(dr, 0))
        )
        close[n].start()
    for copy in close:
        copy.wait_recv()
    summed = sums_ref[:, share(0)].astype(F32) + shares[0].astype(F32) + shares[1].astype(F32)
    reduced[...] = summed.astype(BF16)

    def to_col(n):
        other = lax.rem(col + n, COLS)
        return pltpu.make_async_remote_copy(
            src_ref=reduced.at[pl.ds(pl.multiple_of(other * 16, 16), 16)],
            dst_ref=landed.at[col],
            send_sem=col_send.at[n],
            recv_sem=col_recv.at[n],
            device_id=(row, other),
            device_id_type=MESH,
        )

    def start_col(n, carry):
        to_col(n).start()
        return carry

    lax.fori_loop(1, COLS, start_col, 0)
    landed[col] = reduced[pl.ds(pl.multiple_of(col * 16, 16), 16), :]

    def wait_col(n, carry):
        to_col(n).wait()
        return carry

    lax.fori_loop(1, COLS, wait_col, 0)
    second = None
    for h in range(2):
        slots = jnp.concatenate([landed[2 * k + h] for k in range(16)], axis=0)
        chosen = jnp.dot(select, slots, preferred_element_type=F32)
        hidden = jnp.maximum(chosen + first_bias_ref[row, h : h + 1, :], 0.0).astype(BF16)
        part = jnp.dot(hidden, second_rows[h], preferred_element_type=F32)
        second = part if second is None else second + part
    parts[...] = second.astype(BF16)
    copies = [
        pltpu.make_async_remote_copy(
            src_ref=parts.at[:, pl.ds(pl.multiple_of(other * 256, 256), 256)],
            dst_ref=final.at[n],
            send_sem=last_send.at[n],
            recv_sem=last_recv.at[n],
            device_id=(other, col),
            device_id_type=MESH,
        )
        for n, other in enumerate(rows_near)
    ]
    for copy in copies:
        copy.start()
    for copy in copies:
        copy.wait()
    summed = parts[:, pl.ds(pl.multiple_of(row * 256, 256), 256)].astype(F32)
    for n in range(ROWS - 1):
        summed = summed + final[n].astype(F32)
    out_ref[...] = jnp.maximum(summed + second_bias_ref[pl.ds(row, 1), :], 0.0).astype(BF16)
    for stage in stages:
        for copy in stage:
            copy.wait_send()
    for copy in swaps + pairs + far + close:
        copy.wait_send()
    features_out.wait()


def whole(
    tokens,
    project_in,
    project_out,
    expand_weight,
    reduce_weight,
    first_weight,
    tiles,
    codes,
    first_bias,
    second_weight,
    second_bias,
):
    anywhere = pl.BlockSpec(memory_space=pl.ANY)
    dma = pltpu.SemaphoreType.DMA
    halo_count = len(HALO_COPIES)
    return pl.pallas_call(
        whole_kernel,
        out_shape=(
            jax.ShapeDtypeStruct((SIDE, SIDE, D), BF16),
            jax.ShapeDtypeStruct((128, 256), BF16),
        ),
        in_specs=[VMEM_SPEC]
        + [anywhere] * 5
        + [VMEM_SPEC] * 3
        + [anywhere, VMEM_SPEC],
        out_specs=(anywhere, VMEM_SPEC),
        scratch_shapes=[
            pltpu.VMEM((OWN, D), BF16),
            pltpu.VMEM((HALO, D), BF16),
            pltpu.VMEM((D, 3 * D), BF16),
            pltpu.VMEM((D, D), BF16),
            pltpu.VMEM((D, MLP), BF16),
            pltpu.VMEM((MLP, D), BF16),
            pltpu.VMEM((OWN, 2 * D), BF16),
            pltpu.VMEM((HALO, 2 * D), BF16),
            pltpu.VMEM((OWN, D), F32),
            pltpu.VMEM((OWN, D), F32),
            pltpu.VMEM((6, SIDE, 32, 128), F32),
            pltpu.VMEM((224, D), F32),
            pltpu.VMEM((SIDE, SIDE, D), BF16),
            pltpu.VMEM((49, UNITS, 192), BF16),
            pltpu.VMEM((4, 4, TILES, UNITS, 128), BF16),
            pltpu.VMEM((ROWS, 112, 384), BF16),
            pltpu.VMEM((2, ROWS, 112, 384), BF16),
            pltpu.VMEM((8, 256, 256), BF16),
            pltpu.VMEM((8, 64, 128), jnp.int32),
            pltpu.VMEM((512, D), BF16),
            pltpu.VMEM((512, 512), BF16),
            pltpu.VMEM((2, 512, 128), BF16),
            pltpu.VMEM((2, 256, 128), BF16),
            pltpu.VMEM((2, 512, 128), BF16),
            pltpu.VMEM((512, 128), BF16),
            pltpu.VMEM((COLS, 16, 128), BF16),
            pltpu.VMEM((128, FC), BF16),
            pltpu.VMEM((ROWS - 1, 128, 256), BF16),
            pltpu.VMEM((2, 128, FC), BF16),
            dma((13,)),
            dma((halo_count,)),
            dma((halo_count,)),
            dma((GATHER,)),
            dma((GATHER,)),
            dma,
            dma((ROWS - 1,)),
            dma((ROWS - 1,)),
            dma((ROWS,)),
            dma((ROWS,)),
            dma((4,)),
            dma((4,)),
            dma((COLS,)),
            dma((COLS,)),
            dma((ROWS - 1,)),
            dma((ROWS - 1,)),
        ],
        compiler_params=pltpu.CompilerParams(
            collective_id=0, has_side_effects=True, vmem_limit_bytes=62 * 1024 * 1024
        ),
        cost_estimate=pl.CostEstimate(
            flops=27_000_000_000, bytes_accessed=34_000_000, transcendentals=6_000_000
        ),
        name="whole",
    )(
        tokens,
        project_in,
        project_out,
        expand_weight,
        reduce_weight,
        first_weight,
        tiles,
        codes,
        first_bias,
        second_weight,
        second_bias,
    )


def shards(
    tokens,
    project_in,
    project_out,
    expand_weight,
    reduce_weight,
    first_weight,
    first_bias,
    second_weight,
    second_bias,
    box_tile,
    box_shape,
):
    tiles = box_tile.reshape(COLS, 128)
    codes = (
        (box_shape[:, 0] * 16 + box_shape[:, 1]) * 4
        + (box_shape[:, 2] - 1) * 2
        + (box_shape[:, 3] - 1)
    ).reshape(COLS, 128)
    bias = first_bias.reshape(ROWS, 4, 2, 32).transpose(0, 2, 1, 3).reshape(ROWS, 2, 128)
    features, box_features = whole(
        tokens,
        project_in,
        project_out,
        expand_weight,
        reduce_weight,
        first_weight.transpose(0, 2, 1),
        tiles,
        codes,
        bias,
        second_weight,
        second_bias.reshape(ROWS, 256),
    )
    return (features, box_features)


def solution(mesh):
    return jax.shard_map(
        shards,
        mesh=mesh,
        in_specs=(
            P("row", "col", None),
            P(),
            P(),
            P(),
            P(),
            P(None, "row", "col"),
            P(),
            P(),
            P(),
            P(),
            P(),
        ),
        out_specs=(P("row", "col", None), P("col", "row")),
        check_vma=False,
    )
```

```python
import jax
import jax.numpy as jnp
from jax import lax
from jax.experimental import pallas as pl
from jax.experimental.pallas import tpu as pltpu
from jax.sharding import PartitionSpec as P

ROWS = 4
COLS = 32
D = 768
SIDE = 28
HEADS = 12
MLP = 3072
FC = 1024
S0, S1, S2, OWN = 0, 224, 672, 896
TOP, BOT, LEFT, RIGHT, TL, TR, BL, BR, HALO = 0, 256, 512, 736, 960, 1024, 1088, 1152, 1216
HALO_COPIES = (
    (S0 + 160, 64, TOP, 1, 0),
    (S1 + 320, 128, TOP + 64, 1, 0),
    (S2 + 160, 64, TOP + 192, 1, 0),
    (S0, 64, BOT, -1, 0),
    (S1, 128, BOT + 64, -1, 0),
    (S2, 64, BOT + 192, -1, 0),
    (S2, 224, LEFT, 0, 1),
    (S0, 224, RIGHT, 0, -1),
    (S2 + 160, 64, TL, 1, 1),
    (S0 + 160, 64, TR, 1, -1),
    (S2, 64, BL, -1, 1),
    (S0, 64, BR, -1, -1),
)
QUADS = 12
TILES = 6 * QUADS + 2
HALVES = ((0, 36), (36, 38))
QUARTERS = ((0, 18), (18, 18), (36, 18), (54, 20))
GATHER = 49
UNITS = 32
MESH = pl.DeviceIdType.MESH
F32 = jnp.float32
BF16 = jnp.bfloat16
VMEM_SPEC = pl.BlockSpec(memory_space=pltpu.VMEM)


def norm(values):
    center = values - jnp.mean(values, axis=-1, keepdims=True)
    spread = jnp.mean(center * center, axis=-1, keepdims=True)
    return (center * lax.rsqrt(spread + 1e-6)).astype(BF16)


def window_keys(wy, wx):
    strips = (
        ((False, S0, 8, TOP, BOT), (True, LEFT, 8, TL, BL)),
        ((False, S1, 16, TOP + 64, BOT + 64),),
        ((False, S2, 8, TOP + 192, BOT + 192), (True, RIGHT, 8, TR, BR)),
    )[wx]
    pieces = []
    for outer, base, cells, top, bottom in strips:
        if wy == 0:
            pieces += [(outer, base, 8 * cells), (True, top, 8 * cells)]
        elif wy == 1:
            pieces += [(outer, base + 6 * cells, 16 * cells)]
        else:
            pieces += [(outer, base + 20 * cells, 8 * cells), (True, bottom, 8 * cells)]
    return pieces


def window_bias(wy, wx, row, col):
    lane = lax.broadcasted_iota(jnp.int32, (1, 256), 1)
    cells = 16 if wx == 1 else 8
    line = lax.rem(lane // cells, 16)
    cell = lax.rem(lane, cells)
    if wx == 1:
        keep = cell < 14
    else:
        own_spare, outer_spare = (7, 0) if wx == 0 else (0, 7)
        there = col > 0 if wx == 0 else col < COLS - 1
        keep = ((lane < 128) & (cell != own_spare)) | (
            (lane >= 128) & (cell != outer_spare) & there
        )
    if wy == 0:
        keep = keep & ((line < 7) | ((line > 8) & (row > 0)))
    elif wy == 1:
        keep = keep & (line > 0) & (line < 15)
    else:
        keep = keep & (((line > 0) & (line < 8)) | ((line >= 8) & (line < 15) & (row < ROWS - 1)))
    return jnp.where(keep, 0.0, -1e30).astype(F32)


QUERY_ROWS = [
    ((S0, 56), (S1, 112), (S2, 56)),
    ((S0 + 56, 112), (S1 + 112, 224), (S2 + 56, 112)),
    ((S0 + 168, 56), (S1 + 336, 112), (S2 + 168, 56)),
]


def gather_stages(row, col, whole_ref, send_sem, recv_sem):
    z, y, core = col // 8, lax.rem(col // 2, 4), lax.rem(col, 2)
    numbers = iter(range(GATHER))

    def send(to, place):
        n = next(numbers)
        return pltpu.make_async_remote_copy(
            src_ref=whole_ref.at[place],
            dst_ref=whole_ref.at[place],
            send_sem=send_sem.at[n],
            recv_sem=recv_sem.at[n],
            device_id=(row, to),
            device_id_type=MESH,
        )

    def device(dz, dy):
        return lax.rem(z + dz + 4, 4) * 8 + lax.rem(y + dy + 4, 4) * 2 + core

    def step(at, by):
        return lax.rem(at + by + 4, 4)

    def chunk(axis, first, second):
        dz, dy = (second, first) if axis == 0 else (first, second)
        return step(z, dz), step(y, dy)

    first_to = [{1: device(0, 1), -1: device(0, -1)}, {1: device(1, 0), -1: device(-1, 0)}]
    second_to = first_to[::-1]

    def part(axis, sign):
        return QUARTERS[2 * axis + (0 if sign == 1 else 1)]

    both = [(axis, sign) for axis in range(2) for sign in (1, -1)]
    stages = {n: [] for n in ("own", "cross", "on", "near", "far", "over", "last", "end")}
    for axis, sign in both:
        whole = pl.ds(*HALVES[axis])
        stages["own"].append(send(first_to[axis][sign], (*chunk(axis, 0, 0), whole)))
    for axis, sign in both:
        whole = pl.ds(*HALVES[axis])
        stages["cross"].append(send(second_to[axis][sign], (*chunk(axis, 0, 0), whole)))
    for axis, sign in both:
        place = (*chunk(axis, -sign, 0), pl.ds(*part(axis, sign)))
        stages["on"].append(send(first_to[axis][sign], place))
    for off in (1, -1):
        for axis, sign in both:
            place = (*chunk(axis, off, 0), pl.ds(*HALVES[axis]))
            stages["near"].append(send(second_to[axis][sign], place))
    for axis, sign in both:
        place = (*chunk(axis, 0, -sign), pl.ds(*part(axis, sign)))
        stages["far"].append(send(second_to[axis][sign], place))
    for axis, sign in both:
        place = (*chunk(axis, 2, 0), pl.ds(*HALVES[axis]))
        stages["over"].append(send(second_to[axis][sign], place))
    for off in (1, -1):
        for axis, sign in both:
            place = (*chunk(axis, off, -sign), pl.ds(*part(axis, sign)))
            stages["last"].append(send(second_to[axis][sign], place))
    for n in range(3):
        for axis, sign in both:
            place = (*chunk(axis, 2, -sign), pl.ds(part(axis, sign)[0] + 6 * n, 6))
            stages["end"].append(send(second_to[axis][sign], place))
    stages["end"].append(send(second_to[1][-1], (*chunk(1, 2, 1), pl.ds(6 * QUADS, 2))))
    return stages


def whole_kernel(
    tokens_ref,
    project_in_hbm,
    project_out_hbm,
    expand_hbm,
    reduce_hbm,
    part_hbm,
    tile_ref,
    shape_ref,
    first_bias_ref,
    second_hbm,
    second_bias_ref,
    features_ref,
    out_ref,
    own_ref,
    halo_ref,
    project_in_ref,
    project_out_ref,
    expand_ref,
    reduce_ref,
    kv_own_ref,
    kv_halo_ref,
    query_ref,
    mixed_ref,
    wide_ref,
    small_ref,
    part_ref,
    whole_ref,
    pooled_ref,
    packed_ref,
    group_ref,
    code_ref,
    code_at,
    crops,
    sums_ref,
    ahead_ref,
    passed,
    shares,
    reduced,
    landed,
    parts,
    final,
    second_rows,
    load_sem,
    halo_send,
    halo_recv,
    gather_send,
    gather_recv,
    swap_send,
    swap_recv,
    pair_send,
    pair_recv,
    row_send,
    row_recv,
    col_send,
    col_recv,
    last_send,
    last_recv,
):
    row, col = lax.axis_index("row"), lax.axis_index("col")
    core = lax.rem(col, 2)
    rows_near = [lax.rem(row + n, ROWS) for n in range(1, ROWS)]
    base = col - core
    stages = gather_stages(row, col, whole_ref, gather_send, gather_recv)

    def remote(source, target, send, recv, to):
        return pltpu.make_async_remote_copy(
            src_ref=source,
            dst_ref=target,
            send_sem=send,
            recv_sem=recv,
            device_id=to,
            device_id_type=MESH,
        )

    def near(dr, dc):
        return lax.rem(row + dr + ROWS, ROWS), lax.rem(col + dc + COLS, COLS)

    barrier = pltpu.get_barrier_semaphore()
    greeted = [near(dr, dc) for dr in (-1, 1) for dc in (-1, 0, 1)] + [near(2, 0)]
    for peer in greeted:
        pl.semaphore_signal(barrier, inc=1, device_id=peer, device_id_type=MESH)

    def greet_col(n, carry):
        pl.semaphore_signal(barrier, inc=1, device_id=near(0, n), device_id_type=MESH)
        return carry

    lax.fori_loop(1, COLS, greet_col, 0)
    loads = [
        pltpu.make_async_copy(source, target, load_sem.at[n])
        for n, (source, target) in enumerate(
            [
                (part_hbm, part_ref),
                (project_in_hbm, project_in_ref),
                (project_out_hbm, project_out_ref),
                (expand_hbm, expand_ref),
                (reduce_hbm, reduce_ref),
            ]
            + [
                (
                    second_hbm.at[pl.ds(row * 256 + k * 64 + h * 32, 32)],
                    second_rows.at[h, pl.ds(k * 32, 32)],
                )
                for h in range(2)
                for k in range(4)
            ]
        )
    ]
    for load in loads:
        load.start()
    for y in range(0, SIDE, 2):
        for a in range(2):
            wide_ref[0:6, a, 0:SIDE, :] = jnp.stack(
                [
                    tokens_ref[y + a, :, n * 128 : (n + 1) * 128].astype(F32)
                    for n in range(6)
                ]
            )
        for strip, cells, x in ((S0, 8, 0), (S1, 16, 7), (S2, 8, 20)):
            own_ref[strip + y * cells : strip + (y + 2) * cells, :] = jnp.concatenate(
                [
                    jnp.concatenate(
                        [wide_ref[n, a, x : x + cells, :] for n in range(6)], axis=1
                    )
                    for a in range(2)
                ],
                axis=0,
            ).astype(BF16)
    pl.semaphore_wait(barrier, len(greeted) + COLS - 1)
    halo_copies = [
        remote(
            own_ref.at[pl.ds(src, rows)],
            halo_ref.at[pl.ds(dst, rows)],
            halo_send.at[n],
            halo_recv.at[n],
            near(dr, dc),
        )
        for n, (src, rows, dst, dr, dc) in enumerate(HALO_COPIES)
    ]
    for copy in halo_copies:
        copy.start()

    z, y = col // 8, lax.rem(col // 2, 4)
    loads[0].wait()

    def pack(q, carry):
        four = [part_ref[4 * q + m].astype(F32) for m in range(4)]
        for m in range(4):
            whole_ref[z, y, 6 * q + m] = four[m][:, :128].astype(BF16)
        for m in range(2):
            whole_ref[z, y, 6 * q + 4 + m] = jnp.concatenate(
                [four[2 * m][:, 128:], four[2 * m + 1][:, 128:]], axis=1
            ).astype(BF16)
        return carry

    lax.fori_loop(0, QUADS, pack, 0)
    last = part_ref[4 * QUADS].astype(F32)
    whole_ref[z, y, 6 * QUADS] = last[:, :128].astype(BF16)
    whole_ref[z, y, 6 * QUADS + 1] = jnp.concatenate(
        [last[:, 128:], jnp.zeros((UNITS, 64), F32)], axis=1
    ).astype(BF16)
    for copy in stages["own"] + stages["cross"]:
        copy.start()

    loads[1].wait()

    def project_own(n, carry):
        at = pl.ds(pl.multiple_of(n * 224, 224), 224)
        normed = norm(own_ref[at, :].astype(F32))
        query_ref[at, :] = (
            jnp.dot(normed, project_in_ref[:, :D], preferred_element_type=F32)
            .astype(BF16)
            .astype(F32)
            * 0.125
        )
        kv_own_ref[at, :] = jnp.dot(
            normed, project_in_ref[:, D:], preferred_element_type=F32
        ).astype(BF16)
        return carry

    lax.fori_loop(0, 4, project_own, 0)
    left_half = lax.broadcasted_iota(jnp.int32, (1, 128), 1) < 64
    ones = jnp.ones((256, 128), BF16)

    def attend(wy, wx):
        start, rows = QUERY_ROWS[wy][wx]
        bias = window_bias(wy, wx, row, col)
        pieces = window_keys(wy, wx)
        for h in range(HEADS // 2):
            lanes = slice(h * 128, (h + 1) * 128)
            asked = query_ref[start : start + rows, lanes]
            both = jnp.concatenate(
                [jnp.where(left_half, asked, 0.0), jnp.where(left_half, 0.0, asked)],
                axis=0,
            ).astype(BF16)

            def read(first, pieces=pieces):
                return jnp.concatenate(
                    [
                        (kv_halo_ref if outer else kv_own_ref)[
                            place : place + count, first : first + 128
                        ]
                        for outer, place, count in pieces
                    ],
                    axis=0,
                )

            scores = (
                lax.dot_general(
                    both,
                    read(h * 128),
                    (((1,), (1,)), ((), ())),
                    preferred_element_type=F32,
                )
                + bias
            )
            weights = jnp.exp(scores - jnp.max(scores, axis=-1, keepdims=True)).astype(BF16)
            values = jnp.concatenate([read(D + h * 128), ones], axis=1)
            mixed = jnp.dot(weights, values, preferred_element_type=F32)
            mixed = mixed[:, :128] / mixed[:, 128:]
            mixed_ref[start : start + rows, lanes] = jnp.where(
                left_half, mixed[:rows], mixed[rows:]
            )

    def finish(spans):
        after = jnp.concatenate(
            [own_ref[first : first + rows, :].astype(F32) for first, rows in spans], axis=0
        ) + jnp.dot(
            jnp.concatenate(
                [mixed_ref[first : first + rows, :].astype(BF16) for first, rows in spans], axis=0
            ),
            project_out_ref[...],
            preferred_element_type=F32,
        )
        normed = norm(after)
        total = after
        for part in range(MLP // D):
            units = slice(part * D, (part + 1) * D)
            hidden = jax.nn.gelu(
                jnp.dot(normed, expand_ref[:, units], preferred_element_type=F32)
            ).astype(BF16)
            total = total + jnp.dot(hidden, reduce_ref[units, :], preferred_element_type=F32)
        total = total.astype(BF16).astype(F32)
        done = 0
        for first, rows in spans:
            mixed_ref[first : first + rows, :] = total[done : done + rows]
            done += rows

    attend(1, 1)
    for load in loads[2:]:
        load.wait()
    finish(((S1 + 112, 224),))
    for copy in stages["own"]:
        copy.wait_recv()
    for copy in stages["on"] + stages["near"]:
        copy.start()

    for c in range(COLS):
        lanes = slice(c * 128, (c + 1) * 128)
        code_ref[c : c + 1, :] = (
            (shape_ref[0:1, lanes] * 16 + shape_ref[1:2, lanes]) * 4
            + (shape_ref[2:3, lanes] - 1) * 2
            + (shape_ref[3:4, lanes] - 1)
        )

    lane = lax.broadcasted_iota(jnp.int32, (COLS, 128), 1)
    for t in range(8):
        here = tile_ref[...] == t // 2 * COLS + base + t % 2
        first = jnp.min(jnp.where(here, lane, 127), axis=1, keepdims=True)
        last = jnp.max(jnp.where(here, lane, 0), axis=1, keepdims=True)
        for rank, pick in enumerate((first, last)):
            code = jnp.sum(jnp.where(lane == pick, code_ref[...], 0), axis=1, keepdims=True)
            code_at[t, rank * COLS : (rank + 1) * COLS, :] = jnp.broadcast_to(code, (COLS, 128))

    tiles = tile_ref[pl.ds(col, 1), :]
    down = lax.broadcasted_iota(jnp.int32, (128, 128), 0)
    across = lax.broadcasted_iota(jnp.int32, (128, 128), 1)
    spread = jnp.broadcast_to(tiles, (128, 128))
    mine = jnp.sum(jnp.where(down == across, spread, 0), axis=1, keepdims=True)
    earlier = jnp.where((mine == spread) & (across < down), 1, 0)
    rank = jnp.max(earlier, axis=1, keepdims=True)
    tile_col = lax.rem(mine, COLS)
    slot = tile_col // 2 * 16 + (mine // COLS * 2 + lax.rem(tile_col, 2)) * 2 + rank
    select = (
        (slot == lax.broadcasted_iota(jnp.int32, (128, 256), 1)).astype(F32).astype(BF16)
    )
    to = lax.broadcasted_iota(jnp.int32, (512, 512), 0)
    source = lax.rem(to // 2, 8) * 64 + lax.rem(to, 2) * 32 + to // 16
    order = (source == lax.broadcasted_iota(jnp.int32, (512, 512), 1)).astype(F32).astype(BF16)

    for copy in halo_copies:
        copy.wait()

    def project_halo(n, carry):
        at = pl.ds(pl.multiple_of(n * 304, 304), 304)
        normed = norm(halo_ref[at, :].astype(F32))
        kv_halo_ref[at, :] = jnp.dot(
            normed, project_in_ref[:, D:], preferred_element_type=F32
        ).astype(BF16)
        return carry

    lax.fori_loop(0, 4, project_halo, 0)
    for copy in stages["cross"]:
        copy.wait_recv()
    for copy in stages["far"]:
        copy.start()

    for wy in range(3):
        for wx in range(3):
            if (wy, wx) != (1, 1):
                attend(wy, wx)

    for copy in stages["on"]:
        copy.wait_recv()
    for copy in stages["over"]:
        copy.start()

    wide_ref[:, :, SIDE:, :] = jnp.zeros((6, SIDE, 32 - SIDE, 128), F32)

    def place_row(y, carry):
        for n in range(6):
            lanes = slice(n * 128, (n + 1) * 128)
            wide_ref[n, y, 0:8, :] = mixed_ref[pl.ds(pl.multiple_of(S0 + y * 8, 8), 8), lanes]
            wide_ref[n, y, 20:28, :] = mixed_ref[pl.ds(pl.multiple_of(S2 + y * 8, 8), 8), lanes]
            middle = mixed_ref[pl.ds(pl.multiple_of(S1 + y * 16, 16), 16), lanes]
            wide_ref[n, y, 7:21, :] = middle[:14]
        features_ref[y] = jnp.concatenate(
            [wide_ref[n, y, 0:SIDE, :] for n in range(6)], axis=1
        ).astype(BF16)
        return carry

    def pool(u, carry):
        for n in range(6):
            total = (
                wide_ref[n, 2 * u, pl.ds(0, 16, stride=2), :]
                + wide_ref[n, 2 * u, pl.ds(1, 16, stride=2), :]
                + wide_ref[n, 2 * u + 1, pl.ds(0, 16, stride=2), :]
                + wide_ref[n, 2 * u + 1, pl.ds(1, 16, stride=2), :]
            )
            small_ref[pl.ds(pl.multiple_of(u * 16, 16), 16), n * 128 : (n + 1) * 128] = (
                total * 0.25
            )
        return carry

    near_half = lax.broadcasted_iota(jnp.int32, (64, 128), 1) < 64

    def pack_pooled(half):
        for group, first in enumerate((0, 128, 384, 512)):
            values = small_ref[half * 112 : half * 112 + 112, first : first + 256]
            if group % 2:
                values = pltpu.roll(values, 192, 1)
            upper, lower = values[:64], values[48:]
            rest = jnp.where(near_half, upper[:, 128:], pltpu.roll(lower[:, 128:], 64, 1))
            pooled_ref[half, group] = jnp.concatenate(
                [upper[:, :128], lower[:, :128], rest], axis=1
            ).astype(BF16)

    def to_row(half, n):
        other = lax.rem(row + n, ROWS)
        return remote(
            pooled_ref.at[half, other],
            packed_ref.at[half, core, row],
            swap_send.at[half * 3 + n - 1],
            swap_recv.at[half * 3 + n - 1],
            (other, col),
        )

    def to_pair(half, n):
        there = lax.rem(row - n + ROWS, ROWS)
        return remote(
            packed_ref.at[half, core, there],
            packed_ref.at[half, core, there],
            pair_send.at[half * 4 + n],
            pair_recv.at[half * 4 + n],
            (row, base + 1 - core),
        )

    swaps = [[to_row(half, n) for n in range(1, ROWS)] for half in range(2)]
    pairs = [[to_pair(half, n) for n in range(ROWS)] for half in range(2)]
    for half in range(2):
        finish(((S0 + half * 112, 112), (S1 + half * 336, 112), (S2 + half * 112, 112)))
        if half == 1:
            for copy in stages["near"]:
                copy.wait_recv()
            for copy in stages["last"]:
                copy.start()
        lax.fori_loop(half * 14, half * 14 + 14, place_row, 0)
        lax.fori_loop(half * 7, half * 7 + 7, pool, 0)
        pack_pooled(half)
        for copy in swaps[half]:
            copy.start()
        packed_ref[half, core, row] = pooled_ref[half, row]
        pairs[half][0].start()
    for half in range(2):
        for n in range(1, ROWS):
            swaps[half][n - 1].wait_recv()
            pairs[half][n].start()
    for copy in stages["over"]:
        copy.wait_recv()
    for copy in stages["end"]:
        copy.start()
    swaps = swaps[0] + swaps[1]
    pairs = pairs[0] + pairs[1]
    for copy in pairs:
        copy.wait_recv()

    group_ref[:, 224:, :] = jnp.zeros((8, 32, 256), BF16)
    for half in range(2):
        top = half * 112
        for t in range(8):
            packed = packed_ref[half, t % 2, t // 2].astype(F32)
            rest = packed[:, 256:]
            turned = pltpu.roll(rest, 64, 1)
            group_ref[t, top : top + 64, :] = jnp.concatenate(
                [packed[:, :128], jnp.where(near_half, rest, turned)], axis=1
            ).astype(BF16)
            group_ref[t, top + 48 : top + 112, :] = jnp.concatenate(
                [packed[:, 128:256], jnp.where(near_half, turned, rest)], axis=1
            ).astype(BF16)

    spot = lax.broadcasted_iota(jnp.int32, (64, 128), 1)
    near_lanes = spot < 64

    def sample(t, bins):
        code = code_at[t]
        below = 16 * (1 + lax.rem(code // 2, 2))
        right = 1 + lax.rem(code, 2)
        picks = []
        for bin in bins:
            position = code // 4 + (bin // 7) * below + (bin % 7) * right
            low = (position == spot).astype(F32)
            high = (position == spot + 128).astype(F32)
            picks.append(jnp.concatenate([low, high], axis=1).astype(BF16))
        return jnp.dot(
            jnp.concatenate(picks, axis=0), group_ref[t], preferred_element_type=F32
        )

    def multiply(width, tile):
        weight = jnp.concatenate(
            [whole_ref[:, :, tile + n].reshape(16 * UNITS, 128) for n in range(width)], axis=1
        )
        return lax.dot_general(
            crops[:, : 128 * width],
            weight,
            (((1,), (1,)), ((), ())),
            preferred_element_type=F32,
        )

    for copy in stages["far"] + stages["last"] + stages["end"][12:]:
        copy.wait_recv()
    for t in range(8):
        crops[t * 64 : (t + 1) * 64, :256] = sample(t, (4 * QUADS,)).astype(BF16)
    total = mixed_ref.at[0:512, 0:512]
    total[...] = multiply(2, 6 * QUADS)
    for n in range(3):
        for quarter in range(4):
            quad = 3 * quarter + n
            for t in range(8):
                found = sample(t, range(4 * quad, 4 * quad + 4))
                for m in range(4):
                    crops[t * 64 : (t + 1) * 64, m * 128 : (m + 1) * 128] = found[
                        m * 64 : (m + 1) * 64, :128
                    ].astype(BF16)
                for m in range(2):
                    crops[t * 64 : (t + 1) * 64, (4 + m) * 128 : (5 + m) * 128] = jnp.where(
                        near_lanes,
                        found[m * 128 : m * 128 + 64, 128:],
                        found[m * 128 + 64 : m * 128 + 128, 128:],
                    ).astype(BF16)
            stages["end"][4 * n + quarter].wait_recv()
            total[...] += multiply(6, 6 * quad)
    sums_ref[...] = jnp.dot(
        order, total[...].astype(BF16), preferred_element_type=F32
    ).astype(BF16)

    def share(n):
        return pl.ds(pl.multiple_of(lax.rem(row + n + ROWS, ROWS) * 128, 128), 128)

    sides = ((1, 0), (-1, 256))
    far = [
        remote(
            sums_ref.at[pl.ds(first, 256), share(2)],
            passed.at[n],
            row_send.at[n],
            row_recv.at[n],
            near(dr, 0),
        )
        for n, (dr, first) in enumerate(sides)
    ]
    for copy in far:
        copy.start()
    for copy in far:
        copy.wait_recv()
    close = []
    for n, (dr, first) in enumerate(sides):
        ahead_ref[n] = sums_ref[:, share(dr)]
        ahead_ref[n, first : first + 256, :] = (
            sums_ref[first : first + 256, share(dr)].astype(F32) + passed[n].astype(F32)
        ).astype(BF16)
        close.append(
            remote(ahead_ref.at[n], shares.at[n], row_send.at[2 + n], row_recv.at[2 + n], near(dr, 0))
        )
        close[n].start()
    for copy in close:
        copy.wait_recv()
    summed = sums_ref[:, share(0)].astype(F32) + shares[0].astype(F32) + shares[1].astype(F32)
    reduced[...] = summed.astype(BF16)

    def to_col(n):
        other = lax.rem(col + n, COLS)
        return pltpu.make_async_remote_copy(
            src_ref=reduced.at[pl.ds(pl.multiple_of(other * 16, 16), 16)],
            dst_ref=landed.at[col],
            send_sem=col_send.at[n],
            recv_sem=col_recv.at[n],
            device_id=(row, other),
            device_id_type=MESH,
        )

    def start_col(n, carry):
        to_col(n).start()
        return carry

    lax.fori_loop(1, COLS, start_col, 0)
    landed[col] = reduced[pl.ds(pl.multiple_of(col * 16, 16), 16), :]

    def wait_col(n, carry):
        to_col(n).wait()
        return carry

    lax.fori_loop(1, COLS, wait_col, 0)
    second = None
    for h in range(2):
        slots = jnp.concatenate([landed[2 * k + h] for k in range(16)], axis=0)
        chosen = jnp.dot(select, slots, preferred_element_type=F32)
        bias = jnp.concatenate(
            [
                first_bias_ref[pl.ds(2 * row + n, 1), :][:, 64 * m + 32 * h : 64 * m + 32 * h + 32]
                for n in range(2)
                for m in range(2)
            ],
            axis=1,
        )
        hidden = jnp.maximum(chosen + bias, 0.0).astype(BF16)
        part = jnp.dot(hidden, second_rows[h], preferred_element_type=F32)
        second = part if second is None else second + part
    parts[...] = second.astype(BF16)
    copies = [
        pltpu.make_async_remote_copy(
            src_ref=parts.at[:, pl.ds(pl.multiple_of(other * 256, 256), 256)],
            dst_ref=final.at[n],
            send_sem=last_send.at[n],
            recv_sem=last_recv.at[n],
            device_id=(other, col),
            device_id_type=MESH,
        )
        for n, other in enumerate(rows_near)
    ]
    for copy in copies:
        copy.start()
    for copy in copies:
        copy.wait()
    summed = parts[:, pl.ds(pl.multiple_of(row * 256, 256), 256)].astype(F32)
    for n in range(ROWS - 1):
        summed = summed + final[n].astype(F32)
    bias = jnp.concatenate([second_bias_ref[pl.ds(2 * row + n, 1), :] for n in range(2)], axis=1)
    out_ref[...] = jnp.maximum(summed + bias, 0.0).astype(BF16)
    for stage in stages.values():
        for copy in stage:
            copy.wait_send()
    for copy in swaps + pairs + far + close:
        copy.wait_send()


def whole(
    tokens,
    project_in,
    project_out,
    expand_weight,
    reduce_weight,
    first_weight,
    tiles,
    shapes,
    first_bias,
    second_weight,
    second_bias,
):
    anywhere = pl.BlockSpec(memory_space=pl.ANY)
    dma = pltpu.SemaphoreType.DMA
    halo_count = len(HALO_COPIES)
    return pl.pallas_call(
        whole_kernel,
        out_shape=(
            jax.ShapeDtypeStruct((SIDE, SIDE, D), BF16),
            jax.ShapeDtypeStruct((128, 256), BF16),
        ),
        in_specs=[VMEM_SPEC]
        + [anywhere] * 5
        + [VMEM_SPEC] * 3
        + [anywhere, VMEM_SPEC],
        out_specs=(VMEM_SPEC, VMEM_SPEC),
        scratch_shapes=[
            pltpu.VMEM((OWN, D), BF16),
            pltpu.VMEM((HALO, D), BF16),
            pltpu.VMEM((D, 3 * D), BF16),
            pltpu.VMEM((D, D), BF16),
            pltpu.VMEM((D, MLP), BF16),
            pltpu.VMEM((MLP, D), BF16),
            pltpu.VMEM((OWN, 2 * D), BF16),
            pltpu.VMEM((HALO, 2 * D), BF16),
            pltpu.VMEM((OWN, D), F32),
            pltpu.VMEM((OWN, D), F32),
            pltpu.VMEM((6, SIDE, 32, 128), F32),
            pltpu.VMEM((224, D), F32),
            pltpu.VMEM((49, UNITS, 192), BF16),
            pltpu.VMEM((4, 4, TILES, UNITS, 128), BF16),
            pltpu.VMEM((2, ROWS, 64, 384), BF16),
            pltpu.VMEM((2, 2, ROWS, 64, 384), BF16),
            pltpu.VMEM((8, 256, 256), BF16),
            pltpu.VMEM((COLS, 128), jnp.int32),
            pltpu.VMEM((8, 64, 128), jnp.int32),
            pltpu.VMEM((512, D), BF16),
            pltpu.VMEM((512, 512), BF16),
            pltpu.VMEM((2, 512, 128), BF16),
            pltpu.VMEM((2, 256, 128), BF16),
            pltpu.VMEM((2, 512, 128), BF16),
            pltpu.VMEM((512, 128), BF16),
            pltpu.VMEM((COLS, 16, 128), BF16),
            pltpu.VMEM((128, FC), BF16),
            pltpu.VMEM((ROWS - 1, 128, 256), BF16),
            pltpu.VMEM((2, 128, FC), BF16),
            dma((13,)),
            dma((halo_count,)),
            dma((halo_count,)),
            dma((GATHER,)),
            dma((GATHER,)),
            dma((6,)),
            dma((6,)),
            dma((8,)),
            dma((8,)),
            dma((4,)),
            dma((4,)),
            dma((COLS,)),
            dma((COLS,)),
            dma((ROWS - 1,)),
            dma((ROWS - 1,)),
        ],
        compiler_params=pltpu.CompilerParams(
            collective_id=0, has_side_effects=True, vmem_limit_bytes=54 * 1024 * 1024
        ),
        cost_estimate=pl.CostEstimate(
            flops=27_000_000_000, bytes_accessed=34_000_000, transcendentals=6_000_000
        ),
        name="whole",
    )(
        tokens,
        project_in,
        project_out,
        expand_weight,
        reduce_weight,
        first_weight,
        tiles,
        shapes,
        first_bias,
        second_weight,
        second_bias,
    )


def shards(
    tokens,
    project_in,
    project_out,
    expand_weight,
    reduce_weight,
    first_weight,
    first_bias,
    second_weight,
    second_bias,
    box_tile,
    box_shape,
):
    tiles = box_tile.reshape(COLS, 128)
    features, box_features = whole(
        tokens,
        project_in,
        project_out,
        expand_weight,
        reduce_weight,
        first_weight.transpose(0, 2, 1),
        tiles,
        box_shape.transpose(1, 0),
        first_bias.reshape(8, 128),
        second_weight,
        second_bias.reshape(8, 128),
    )
    return (features, box_features)


def solution(mesh):
    return jax.shard_map(
        shards,
        mesh=mesh,
        in_specs=(
            P("row", "col", None),
            P(),
            P(),
            P(),
            P(),
            P(None, "row", "col"),
            P(),
            P(),
            P(),
            P(),
            P(),
        ),
        out_specs=(P("row", "col", None), P("col", "row")),
        check_vma=False,
    )
```

```python
import jax
import jax.numpy as jnp
from jax import lax
from jax.experimental import pallas as pl
from jax.experimental.pallas import tpu as pltpu
from jax.sharding import PartitionSpec as P

ROWS = 4
COLS = 32
D = 768
SIDE = 28
HEADS = 12
MLP = 3072
FC = 1024
S0, S1, S2, OWN = 0, 224, 672, 896
TOP, BOT, LEFT, RIGHT, TL, TR, BL, BR, HALO = 0, 256, 512, 736, 960, 1024, 1088, 1152, 1216
HALO_COPIES = (
    (S0 + 160, 64, TOP, 1, 0),
    (S1 + 320, 128, TOP + 64, 1, 0),
    (S2 + 160, 64, TOP + 192, 1, 0),
    (S0, 64, BOT, -1, 0),
    (S1, 128, BOT + 64, -1, 0),
    (S2, 64, BOT + 192, -1, 0),
    (S2, 224, LEFT, 0, 1),
    (S0, 224, RIGHT, 0, -1),
    (S2 + 160, 64, TL, 1, 1),
    (S0 + 160, 64, TR, 1, -1),
    (S2, 64, BL, -1, 1),
    (S0, 64, BR, -1, -1),
)
QUADS = 12
TILES = 6 * QUADS + 2
HALVES = ((0, 36), (36, 38))
QUARTERS = ((0, 18), (18, 18), (36, 18), (54, 20))
GATHER = 49
UNITS = 32
MESH = pl.DeviceIdType.MESH
F32 = jnp.float32
BF16 = jnp.bfloat16
VMEM_SPEC = pl.BlockSpec(memory_space=pltpu.VMEM)


def norm(values):
    center = values - jnp.mean(values, axis=-1, keepdims=True)
    spread = jnp.mean(center * center, axis=-1, keepdims=True)
    return (center * lax.rsqrt(spread + 1e-6)).astype(BF16)


def window_keys(wy, wx):
    strips = (
        ((False, S0, 8, TOP, BOT), (True, LEFT, 8, TL, BL)),
        ((False, S1, 16, TOP + 64, BOT + 64),),
        ((False, S2, 8, TOP + 192, BOT + 192), (True, RIGHT, 8, TR, BR)),
    )[wx]
    pieces = []
    for outer, base, cells, top, bottom in strips:
        if wy == 0:
            pieces += [(outer, base, 8 * cells), (True, top, 8 * cells)]
        elif wy == 1:
            pieces += [(outer, base + 6 * cells, 16 * cells)]
        else:
            pieces += [(outer, base + 20 * cells, 8 * cells), (True, bottom, 8 * cells)]
    return pieces


def window_bias(wy, wx, row, col):
    lane = lax.broadcasted_iota(jnp.int32, (1, 256), 1)
    cells = 16 if wx == 1 else 8
    line = lax.rem(lane // cells, 16)
    cell = lax.rem(lane, cells)
    if wx == 1:
        keep = cell < 14
    else:
        own_spare, outer_spare = (7, 0) if wx == 0 else (0, 7)
        there = col > 0 if wx == 0 else col < COLS - 1
        keep = ((lane < 128) & (cell != own_spare)) | (
            (lane >= 128) & (cell != outer_spare) & there
        )
    if wy == 0:
        keep = keep & ((line < 7) | ((line > 8) & (row > 0)))
    elif wy == 1:
        keep = keep & (line > 0) & (line < 15)
    else:
        keep = keep & (((line > 0) & (line < 8)) | ((line >= 8) & (line < 15) & (row < ROWS - 1)))
    return jnp.where(keep, 0.0, -1e30).astype(F32)


QUERY_ROWS = [
    ((S0, 56), (S1, 112), (S2, 56)),
    ((S0 + 56, 112), (S1 + 112, 224), (S2 + 56, 112)),
    ((S0 + 168, 56), (S1 + 336, 112), (S2 + 168, 56)),
]


def gather_stages(row, col, whole_ref, send_sem, recv_sem):
    z, y, core = col // 8, lax.rem(col // 2, 4), lax.rem(col, 2)
    numbers = iter(range(GATHER))

    def send(to, place):
        n = next(numbers)
        return pltpu.make_async_remote_copy(
            src_ref=whole_ref.at[place],
            dst_ref=whole_ref.at[place],
            send_sem=send_sem.at[n],
            recv_sem=recv_sem.at[n],
            device_id=(row, to),
            device_id_type=MESH,
        )

    def device(dz, dy):
        return lax.rem(z + dz + 4, 4) * 8 + lax.rem(y + dy + 4, 4) * 2 + core

    def step(at, by):
        return lax.rem(at + by + 4, 4)

    def chunk(axis, first, second):
        dz, dy = (second, first) if axis == 0 else (first, second)
        return step(z, dz), step(y, dy)

    first_to = [{1: device(0, 1), -1: device(0, -1)}, {1: device(1, 0), -1: device(-1, 0)}]
    second_to = first_to[::-1]

    def part(axis, sign):
        return QUARTERS[2 * axis + (0 if sign == 1 else 1)]

    both = [(axis, sign) for axis in range(2) for sign in (1, -1)]
    stages = {n: [] for n in ("own", "cross", "on", "near", "far", "over", "last", "end")}
    for axis, sign in both:
        whole = pl.ds(*HALVES[axis])
        stages["own"].append(send(first_to[axis][sign], (*chunk(axis, 0, 0), whole)))
    for axis, sign in both:
        whole = pl.ds(*HALVES[axis])
        stages["cross"].append(send(second_to[axis][sign], (*chunk(axis, 0, 0), whole)))
    for axis, sign in both:
        place = (*chunk(axis, -sign, 0), pl.ds(*part(axis, sign)))
        stages["on"].append(send(first_to[axis][sign], place))
    for off in (1, -1):
        for axis, sign in both:
            place = (*chunk(axis, off, 0), pl.ds(*HALVES[axis]))
            stages["near"].append(send(second_to[axis][sign], place))
    for axis, sign in both:
        place = (*chunk(axis, 0, -sign), pl.ds(*part(axis, sign)))
        stages["far"].append(send(second_to[axis][sign], place))
    for axis, sign in both:
        place = (*chunk(axis, 2, 0), pl.ds(*HALVES[axis]))
        stages["over"].append(send(second_to[axis][sign], place))
    for off in (1, -1):
        for axis, sign in both:
            place = (*chunk(axis, off, -sign), pl.ds(*part(axis, sign)))
            stages["last"].append(send(second_to[axis][sign], place))
    for n in range(3):
        for axis, sign in both:
            place = (*chunk(axis, 2, -sign), pl.ds(part(axis, sign)[0] + 6 * n, 6))
            stages["end"].append(send(second_to[axis][sign], place))
    stages["end"].append(send(second_to[1][-1], (*chunk(1, 2, 1), pl.ds(6 * QUADS, 2))))
    return stages


def whole_kernel(
    tokens_ref,
    project_in_hbm,
    project_out_hbm,
    expand_hbm,
    reduce_hbm,
    part_hbm,
    tile_ref,
    shape_ref,
    first_bias_ref,
    second_hbm,
    second_bias_ref,
    features_ref,
    out_ref,
    own_ref,
    halo_ref,
    project_in_ref,
    project_out_ref,
    expand_ref,
    reduce_ref,
    kv_own_ref,
    kv_halo_ref,
    query_ref,
    mixed_ref,
    wide_ref,
    small_ref,
    part_ref,
    whole_ref,
    pooled_ref,
    packed_ref,
    group_ref,
    code_ref,
    code_at,
    crops,
    sums_ref,
    ahead_ref,
    passed,
    shares,
    reduced,
    landed,
    parts,
    final,
    second_rows,
    load_sem,
    halo_send,
    halo_recv,
    gather_send,
    gather_recv,
    swap_send,
    swap_recv,
    pair_send,
    pair_recv,
    row_send,
    row_recv,
    col_send,
    col_recv,
    last_send,
    last_recv,
):
    row, col = lax.axis_index("row"), lax.axis_index("col")
    core = lax.rem(col, 2)
    rows_near = [lax.rem(row + n, ROWS) for n in range(1, ROWS)]
    base = col - core
    stages = gather_stages(row, col, whole_ref, gather_send, gather_recv)

    def remote(source, target, send, recv, to):
        return pltpu.make_async_remote_copy(
            src_ref=source,
            dst_ref=target,
            send_sem=send,
            recv_sem=recv,
            device_id=to,
            device_id_type=MESH,
        )

    def near(dr, dc):
        return lax.rem(row + dr + ROWS, ROWS), lax.rem(col + dc + COLS, COLS)

    barrier = pltpu.get_barrier_semaphore()
    greeted = [near(dr, dc) for dr in (-1, 1) for dc in (-1, 0, 1)] + [near(2, 0)]
    for peer in greeted:
        pl.semaphore_signal(barrier, inc=1, device_id=peer, device_id_type=MESH)

    def greet_col(n, carry):
        pl.semaphore_signal(barrier, inc=1, device_id=near(0, n), device_id_type=MESH)
        return carry

    lax.fori_loop(1, COLS, greet_col, 0)
    loads = [
        pltpu.make_async_copy(source, target, load_sem.at[n])
        for n, (source, target) in enumerate(
            [
                (part_hbm, part_ref),
                (project_in_hbm, project_in_ref),
                (project_out_hbm, project_out_ref),
                (expand_hbm, expand_ref),
                (reduce_hbm, reduce_ref),
            ]
            + [
                (
                    second_hbm.at[pl.ds(row * 256 + k * 64 + h * 32, 32)],
                    second_rows.at[h, pl.ds(k * 32, 32)],
                )
                for h in range(2)
                for k in range(4)
            ]
        )
    ]
    for load in loads:
        load.start()
    for y in range(0, SIDE, 2):
        for a in range(2):
            wide_ref[0:6, a, 0:SIDE, :] = jnp.stack(
                [
                    tokens_ref[y + a, :, n * 128 : (n + 1) * 128].astype(F32)
                    for n in range(6)
                ]
            )
        for strip, cells, x in ((S0, 8, 0), (S1, 16, 7), (S2, 8, 20)):
            own_ref[strip + y * cells : strip + (y + 2) * cells, :] = jnp.concatenate(
                [
                    jnp.concatenate(
                        [wide_ref[n, a, x : x + cells, :] for n in range(6)], axis=1
                    )
                    for a in range(2)
                ],
                axis=0,
            ).astype(BF16)
    z, y = col // 8, lax.rem(col // 2, 4)
    loads[0].wait()

    def pack(q, carry):
        four = [part_ref[4 * q + m].astype(F32) for m in range(4)]
        for m in range(4):
            whole_ref[z, y, 6 * q + m] = four[m][:, :128].astype(BF16)
        for m in range(2):
            whole_ref[z, y, 6 * q + 4 + m] = jnp.concatenate(
                [four[2 * m][:, 128:], four[2 * m + 1][:, 128:]], axis=1
            ).astype(BF16)
        return carry

    lax.fori_loop(0, QUADS, pack, 0)
    last = part_ref[4 * QUADS].astype(F32)
    whole_ref[z, y, 6 * QUADS] = last[:, :128].astype(BF16)
    whole_ref[z, y, 6 * QUADS + 1] = jnp.concatenate(
        [last[:, 128:], jnp.zeros((UNITS, 64), F32)], axis=1
    ).astype(BF16)
    pl.semaphore_wait(barrier, len(greeted) + COLS - 1)
    for copy in stages["own"]:
        copy.start()
    halo_copies = [
        remote(
            own_ref.at[pl.ds(src, rows)],
            halo_ref.at[pl.ds(dst, rows)],
            halo_send.at[n],
            halo_recv.at[n],
            near(dr, dc),
        )
        for n, (src, rows, dst, dr, dc) in enumerate(HALO_COPIES)
    ]
    for copy in halo_copies:
        copy.start()
    for copy in stages["cross"]:
        copy.start()


    loads[1].wait()

    def project_own(n, carry):
        at = pl.ds(pl.multiple_of(n * 224, 224), 224)
        normed = norm(own_ref[at, :].astype(F32))
        query_ref[at, :] = (
            jnp.dot(normed, project_in_ref[:, :D], preferred_element_type=F32)
            .astype(BF16)
            .astype(F32)
            * 0.125
        )
        kv_own_ref[at, :] = jnp.dot(
            normed, project_in_ref[:, D:], preferred_element_type=F32
        ).astype(BF16)
        return carry

    lax.fori_loop(0, 4, project_own, 0)
    left_half = lax.broadcasted_iota(jnp.int32, (1, 128), 1) < 64
    ones = jnp.ones((256, 128), BF16)

    def attend(wy, wx):
        start, rows = QUERY_ROWS[wy][wx]
        bias = window_bias(wy, wx, row, col)
        pieces = window_keys(wy, wx)
        for h in range(HEADS // 2):
            lanes = slice(h * 128, (h + 1) * 128)
            asked = query_ref[start : start + rows, lanes]
            both = jnp.concatenate(
                [jnp.where(left_half, asked, 0.0), jnp.where(left_half, 0.0, asked)],
                axis=0,
            ).astype(BF16)

            def read(first, pieces=pieces):
                return jnp.concatenate(
                    [
                        (kv_halo_ref if outer else kv_own_ref)[
                            place : place + count, first : first + 128
                        ]
                        for outer, place, count in pieces
                    ],
                    axis=0,
                )

            scores = (
                lax.dot_general(
                    both,
                    read(h * 128),
                    (((1,), (1,)), ((), ())),
                    preferred_element_type=F32,
                )
                + bias
            )
            weights = jnp.exp(scores - jnp.max(scores, axis=-1, keepdims=True)).astype(BF16)
            values = jnp.concatenate([read(D + h * 128), ones], axis=1)
            mixed = jnp.dot(weights, values, preferred_element_type=F32)
            mixed = mixed[:, :128] / mixed[:, 128:]
            mixed_ref[start : start + rows, lanes] = jnp.where(
                left_half, mixed[:rows], mixed[rows:]
            )

    def finish(spans):
        after = jnp.concatenate(
            [own_ref[first : first + rows, :].astype(F32) for first, rows in spans], axis=0
        ) + jnp.dot(
            jnp.concatenate(
                [mixed_ref[first : first + rows, :].astype(BF16) for first, rows in spans], axis=0
            ),
            project_out_ref[...],
            preferred_element_type=F32,
        )
        normed = norm(after)
        total = after
        for part in range(MLP // D):
            units = slice(part * D, (part + 1) * D)
            hidden = jax.nn.gelu(
                jnp.dot(normed, expand_ref[:, units], preferred_element_type=F32)
            ).astype(BF16)
            total = total + jnp.dot(hidden, reduce_ref[units, :], preferred_element_type=F32)
        total = total.astype(BF16).astype(F32)
        done = 0
        for first, rows in spans:
            mixed_ref[first : first + rows, :] = total[done : done + rows]
            done += rows

    attend(1, 1)
    for load in loads[2:]:
        load.wait()
    finish(((S1 + 112, 224),))
    for copy in stages["own"]:
        copy.wait_recv()
    for copy in stages["on"] + stages["near"]:
        copy.start()

    for c in range(COLS):
        lanes = slice(c * 128, (c + 1) * 128)
        code_ref[c : c + 1, :] = (
            (shape_ref[0:1, lanes] * 16 + shape_ref[1:2, lanes]) * 4
            + (shape_ref[2:3, lanes] - 1) * 2
            + (shape_ref[3:4, lanes] - 1)
        )

    lane = lax.broadcasted_iota(jnp.int32, (COLS, 128), 1)
    for t in range(8):
        here = tile_ref[...] == t // 2 * COLS + base + t % 2
        first = jnp.min(jnp.where(here, lane, 127), axis=1, keepdims=True)
        last = jnp.max(jnp.where(here, lane, 0), axis=1, keepdims=True)
        for rank, pick in enumerate((first, last)):
            code = jnp.sum(jnp.where(lane == pick, code_ref[...], 0), axis=1, keepdims=True)
            code_at[t, rank * COLS : (rank + 1) * COLS, :] = jnp.broadcast_to(code, (COLS, 128))

    tiles = tile_ref[pl.ds(col, 1), :]
    down = lax.broadcasted_iota(jnp.int32, (128, 128), 0)
    across = lax.broadcasted_iota(jnp.int32, (128, 128), 1)
    spread = jnp.broadcast_to(tiles, (128, 128))
    mine = jnp.sum(jnp.where(down == across, spread, 0), axis=1, keepdims=True)
    earlier = jnp.where((mine == spread) & (across < down), 1, 0)
    rank = jnp.max(earlier, axis=1, keepdims=True)
    tile_col = lax.rem(mine, COLS)
    slot = tile_col // 2 * 16 + (mine // COLS * 2 + lax.rem(tile_col, 2)) * 2 + rank
    select = (
        (slot == lax.broadcasted_iota(jnp.int32, (128, 256), 1)).astype(F32).astype(BF16)
    )
    to = lax.broadcasted_iota(jnp.int32, (512, 512), 0)
    source = lax.rem(to // 2, 8) * 64 + lax.rem(to, 2) * 32 + to // 16
    order = (source == lax.broadcasted_iota(jnp.int32, (512, 512), 1)).astype(F32).astype(BF16)

    for copy in halo_copies:
        copy.wait()

    def project_halo(n, carry):
        at = pl.ds(pl.multiple_of(n * 304, 304), 304)
        normed = norm(halo_ref[at, :].astype(F32))
        kv_halo_ref[at, :] = jnp.dot(
            normed, project_in_ref[:, D:], preferred_element_type=F32
        ).astype(BF16)
        return carry

    lax.fori_loop(0, 4, project_halo, 0)
    for copy in stages["cross"]:
        copy.wait_recv()
    for copy in stages["far"]:
        copy.start()

    for wy in range(3):
        for wx in range(3):
            if (wy, wx) != (1, 1):
                attend(wy, wx)

    for copy in stages["on"]:
        copy.wait_recv()
    for copy in stages["over"]:
        copy.start()

    wide_ref[:, :, SIDE:, :] = jnp.zeros((6, SIDE, 32 - SIDE, 128), F32)

    def place_row(y, carry):
        for n in range(6):
            lanes = slice(n * 128, (n + 1) * 128)
            wide_ref[n, y, 0:8, :] = mixed_ref[pl.ds(pl.multiple_of(S0 + y * 8, 8), 8), lanes]
            wide_ref[n, y, 20:28, :] = mixed_ref[pl.ds(pl.multiple_of(S2 + y * 8, 8), 8), lanes]
            middle = mixed_ref[pl.ds(pl.multiple_of(S1 + y * 16, 16), 16), lanes]
            wide_ref[n, y, 7:21, :] = middle[:14]
        features_ref[y] = jnp.concatenate(
            [wide_ref[n, y, 0:SIDE, :] for n in range(6)], axis=1
        ).astype(BF16)
        return carry

    def pool(u, carry):
        for n in range(6):
            total = (
                wide_ref[n, 2 * u, pl.ds(0, 16, stride=2), :]
                + wide_ref[n, 2 * u, pl.ds(1, 16, stride=2), :]
                + wide_ref[n, 2 * u + 1, pl.ds(0, 16, stride=2), :]
                + wide_ref[n, 2 * u + 1, pl.ds(1, 16, stride=2), :]
            )
            small_ref[pl.ds(pl.multiple_of(u * 16, 16), 16), n * 128 : (n + 1) * 128] = (
                total * 0.25
            )
        return carry

    near_half = lax.broadcasted_iota(jnp.int32, (64, 128), 1) < 64

    def pack_pooled(half):
        for group, first in enumerate((0, 128, 384, 512)):
            values = small_ref[half * 112 : half * 112 + 112, first : first + 256]
            if group % 2:
                values = pltpu.roll(values, 192, 1)
            upper, lower = values[:64], values[48:]
            rest = jnp.where(near_half, upper[:, 128:], pltpu.roll(lower[:, 128:], 64, 1))
            pooled_ref[half, group] = jnp.concatenate(
                [upper[:, :128], lower[:, :128], rest], axis=1
            ).astype(BF16)

    def to_row(half, n):
        other = lax.rem(row + n, ROWS)
        return remote(
            pooled_ref.at[half, other],
            packed_ref.at[half, core, row],
            swap_send.at[half * 3 + n - 1],
            swap_recv.at[half * 3 + n - 1],
            (other, col),
        )

    def to_pair(half, n):
        there = lax.rem(row - n + ROWS, ROWS)
        return remote(
            packed_ref.at[half, core, there],
            packed_ref.at[half, core, there],
            pair_send.at[half * 4 + n],
            pair_recv.at[half * 4 + n],
            (row, base + 1 - core),
        )

    swaps = [[to_row(half, n) for n in range(1, ROWS)] for half in range(2)]
    pairs = [[to_pair(half, n) for n in range(ROWS)] for half in range(2)]
    for half in range(2):
        if half == 1:
            for copy in stages["near"]:
                copy.wait_recv()
            for copy in stages["last"]:
                copy.start()
        finish(((S0 + half * 112, 112), (S1 + half * 336, 112), (S2 + half * 112, 112)))
        if half == 1:
            for copy in stages["over"]:
                copy.wait_recv()
            for copy in stages["end"]:
                copy.start()
        lax.fori_loop(half * 14, half * 14 + 14, place_row, 0)
        lax.fori_loop(half * 7, half * 7 + 7, pool, 0)
        pack_pooled(half)
        for copy in swaps[half]:
            copy.start()
        packed_ref[half, core, row] = pooled_ref[half, row]
        pairs[half][0].start()
    for half in range(2):
        for n in range(1, ROWS):
            swaps[half][n - 1].wait_recv()
            pairs[half][n].start()
    swaps = swaps[0] + swaps[1]
    pairs = pairs[0] + pairs[1]
    for copy in pairs:
        copy.wait_recv()

    group_ref[:, 224:, :] = jnp.zeros((8, 32, 256), BF16)
    for half in range(2):
        top = half * 112
        for t in range(8):
            packed = packed_ref[half, t % 2, t // 2].astype(F32)
            rest = packed[:, 256:]
            turned = pltpu.roll(rest, 64, 1)
            group_ref[t, top : top + 64, :] = jnp.concatenate(
                [packed[:, :128], jnp.where(near_half, rest, turned)], axis=1
            ).astype(BF16)
            group_ref[t, top + 48 : top + 112, :] = jnp.concatenate(
                [packed[:, 128:256], jnp.where(near_half, turned, rest)], axis=1
            ).astype(BF16)

    spot = lax.broadcasted_iota(jnp.int32, (64, 128), 1)
    near_lanes = spot < 64

    def sample(t, bins):
        code = code_at[t]
        below = 16 * (1 + lax.rem(code // 2, 2))
        right = 1 + lax.rem(code, 2)
        picks = []
        for bin in bins:
            position = code // 4 + (bin // 7) * below + (bin % 7) * right
            low = (position == spot).astype(F32)
            high = (position == spot + 128).astype(F32)
            picks.append(jnp.concatenate([low, high], axis=1).astype(BF16))
        return jnp.dot(
            jnp.concatenate(picks, axis=0), group_ref[t], preferred_element_type=F32
        )

    def multiply(width, tile):
        weight = jnp.concatenate(
            [whole_ref[:, :, tile + n].reshape(16 * UNITS, 128) for n in range(width)], axis=1
        )
        return lax.dot_general(
            crops[:, : 128 * width],
            weight,
            (((1,), (1,)), ((), ())),
            preferred_element_type=F32,
        )

    for copy in stages["far"] + stages["last"] + stages["end"][12:]:
        copy.wait_recv()
    for t in range(8):
        crops[t * 64 : (t + 1) * 64, :256] = sample(t, (4 * QUADS,)).astype(BF16)
    total = mixed_ref.at[0:512, 0:512]
    total[...] = multiply(2, 6 * QUADS)
    for n in range(3):
        for quarter in range(4):
            quad = 3 * quarter + n
            for t in range(8):
                found = sample(t, range(4 * quad, 4 * quad + 4))
                for m in range(4):
                    crops[t * 64 : (t + 1) * 64, m * 128 : (m + 1) * 128] = found[
                        m * 64 : (m + 1) * 64, :128
                    ].astype(BF16)
                for m in range(2):
                    crops[t * 64 : (t + 1) * 64, (4 + m) * 128 : (5 + m) * 128] = jnp.where(
                        near_lanes,
                        found[m * 128 : m * 128 + 64, 128:],
                        found[m * 128 + 64 : m * 128 + 128, 128:],
                    ).astype(BF16)
            stages["end"][4 * n + quarter].wait_recv()
            total[...] += multiply(6, 6 * quad)
    sums_ref[...] = jnp.dot(
        order, total[...].astype(BF16), preferred_element_type=F32
    ).astype(BF16)

    def share(n):
        return pl.ds(pl.multiple_of(lax.rem(row + n + ROWS, ROWS) * 128, 128), 128)

    sides = ((1, 0), (-1, 256))
    far = [
        remote(
            sums_ref.at[pl.ds(first, 256), share(2)],
            passed.at[n],
            row_send.at[n],
            row_recv.at[n],
            near(dr, 0),
        )
        for n, (dr, first) in enumerate(sides)
    ]
    for copy in far:
        copy.start()
    for copy in far:
        copy.wait_recv()
    close = []
    for n, (dr, first) in enumerate(sides):
        ahead_ref[n] = sums_ref[:, share(dr)]
        ahead_ref[n, first : first + 256, :] = (
            sums_ref[first : first + 256, share(dr)].astype(F32) + passed[n].astype(F32)
        ).astype(BF16)
        close.append(
            remote(ahead_ref.at[n], shares.at[n], row_send.at[2 + n], row_recv.at[2 + n], near(dr, 0))
        )
        close[n].start()
    for copy in close:
        copy.wait_recv()
    summed = sums_ref[:, share(0)].astype(F32) + shares[0].astype(F32) + shares[1].astype(F32)
    reduced[...] = summed.astype(BF16)

    def to_col(n):
        other = lax.rem(col + n, COLS)
        return pltpu.make_async_remote_copy(
            src_ref=reduced.at[pl.ds(pl.multiple_of(other * 16, 16), 16)],
            dst_ref=landed.at[col],
            send_sem=col_send.at[n],
            recv_sem=col_recv.at[n],
            device_id=(row, other),
            device_id_type=MESH,
        )

    def start_col(n, carry):
        to_col(n).start()
        return carry

    lax.fori_loop(1, COLS, start_col, 0)
    landed[col] = reduced[pl.ds(pl.multiple_of(col * 16, 16), 16), :]

    def wait_col(n, carry):
        to_col(n).wait()
        return carry

    lax.fori_loop(1, COLS, wait_col, 0)
    second = None
    for h in range(2):
        slots = jnp.concatenate([landed[2 * k + h] for k in range(16)], axis=0)
        chosen = jnp.dot(select, slots, preferred_element_type=F32)
        bias = jnp.concatenate(
            [
                first_bias_ref[pl.ds(2 * row + n, 1), :][:, 64 * m + 32 * h : 64 * m + 32 * h + 32]
                for n in range(2)
                for m in range(2)
            ],
            axis=1,
        )
        hidden = jnp.maximum(chosen + bias, 0.0).astype(BF16)
        part = jnp.dot(hidden, second_rows[h], preferred_element_type=F32)
        second = part if second is None else second + part
    parts[...] = second.astype(BF16)
    copies = [
        pltpu.make_async_remote_copy(
            src_ref=parts.at[:, pl.ds(pl.multiple_of(other * 256, 256), 256)],
            dst_ref=final.at[n],
            send_sem=last_send.at[n],
            recv_sem=last_recv.at[n],
            device_id=(other, col),
            device_id_type=MESH,
        )
        for n, other in enumerate(rows_near)
    ]
    for copy in copies:
        copy.start()
    for copy in copies:
        copy.wait()
    summed = parts[:, pl.ds(pl.multiple_of(row * 256, 256), 256)].astype(F32)
    for n in range(ROWS - 1):
        summed = summed + final[n].astype(F32)
    bias = jnp.concatenate([second_bias_ref[pl.ds(2 * row + n, 1), :] for n in range(2)], axis=1)
    out_ref[...] = jnp.maximum(summed + bias, 0.0).astype(BF16)
    for stage in stages.values():
        for copy in stage:
            copy.wait_send()
    for copy in swaps + pairs + far + close:
        copy.wait_send()


def whole(
    tokens,
    project_in,
    project_out,
    expand_weight,
    reduce_weight,
    first_weight,
    tiles,
    shapes,
    first_bias,
    second_weight,
    second_bias,
):
    anywhere = pl.BlockSpec(memory_space=pl.ANY)
    dma = pltpu.SemaphoreType.DMA
    halo_count = len(HALO_COPIES)
    return pl.pallas_call(
        whole_kernel,
        out_shape=(
            jax.ShapeDtypeStruct((SIDE, SIDE, D), BF16),
            jax.ShapeDtypeStruct((128, 256), BF16),
        ),
        in_specs=[VMEM_SPEC]
        + [anywhere] * 5
        + [VMEM_SPEC] * 3
        + [anywhere, VMEM_SPEC],
        out_specs=(VMEM_SPEC, VMEM_SPEC),
        scratch_shapes=[
            pltpu.VMEM((OWN, D), BF16),
            pltpu.VMEM((HALO, D), BF16),
            pltpu.VMEM((D, 3 * D), BF16),
            pltpu.VMEM((D, D), BF16),
            pltpu.VMEM((D, MLP), BF16),
            pltpu.VMEM((MLP, D), BF16),
            pltpu.VMEM((OWN, 2 * D), BF16),
            pltpu.VMEM((HALO, 2 * D), BF16),
            pltpu.VMEM((OWN, D), F32),
            pltpu.VMEM((OWN, D), F32),
            pltpu.VMEM((6, SIDE, 32, 128), F32),
            pltpu.VMEM((224, D), F32),
            pltpu.VMEM((49, UNITS, 192), BF16),
            pltpu.VMEM((4, 4, TILES, UNITS, 128), BF16),
            pltpu.VMEM((2, ROWS, 64, 384), BF16),
            pltpu.VMEM((2, 2, ROWS, 64, 384), BF16),
            pltpu.VMEM((8, 256, 256), BF16),
            pltpu.VMEM((COLS, 128), jnp.int32),
            pltpu.VMEM((8, 64, 128), jnp.int32),
            pltpu.VMEM((512, D), BF16),
            pltpu.VMEM((512, 512), BF16),
            pltpu.VMEM((2, 512, 128), BF16),
            pltpu.VMEM((2, 256, 128), BF16),
            pltpu.VMEM((2, 512, 128), BF16),
            pltpu.VMEM((512, 128), BF16),
            pltpu.VMEM((COLS, 16, 128), BF16),
            pltpu.VMEM((128, FC), BF16),
            pltpu.VMEM((ROWS - 1, 128, 256), BF16),
            pltpu.VMEM((2, 128, FC), BF16),
            dma((13,)),
            dma((halo_count,)),
            dma((halo_count,)),
            dma((GATHER,)),
            dma((GATHER,)),
            dma((6,)),
            dma((6,)),
            dma((8,)),
            dma((8,)),
            dma((4,)),
            dma((4,)),
            dma((COLS,)),
            dma((COLS,)),
            dma((ROWS - 1,)),
            dma((ROWS - 1,)),
        ],
        compiler_params=pltpu.CompilerParams(
            collective_id=0, has_side_effects=True, vmem_limit_bytes=54 * 1024 * 1024
        ),
        cost_estimate=pl.CostEstimate(
            flops=27_000_000_000, bytes_accessed=34_000_000, transcendentals=6_000_000
        ),
        name="whole",
    )(
        tokens,
        project_in,
        project_out,
        expand_weight,
        reduce_weight,
        first_weight,
        tiles,
        shapes,
        first_bias,
        second_weight,
        second_bias,
    )


def shards(
    tokens,
    project_in,
    project_out,
    expand_weight,
    reduce_weight,
    first_weight,
    first_bias,
    second_weight,
    second_bias,
    box_tile,
    box_shape,
):
    tiles = box_tile.reshape(COLS, 128)
    features, box_features = whole(
        tokens,
        project_in,
        project_out,
        expand_weight,
        reduce_weight,
        first_weight.transpose(0, 2, 1),
        tiles,
        box_shape.transpose(1, 0),
        first_bias.reshape(8, 128),
        second_weight,
        second_bias.reshape(8, 128),
    )
    return (features, box_features)


def solution(mesh):
    return jax.shard_map(
        shards,
        mesh=mesh,
        in_specs=(
            P("row", "col", None),
            P(),
            P(),
            P(),
            P(),
            P(None, "row", "col"),
            P(),
            P(),
            P(),
            P(),
            P(),
        ),
        out_specs=(P("row", "col", None), P("col", "row")),
        check_vma=False,
    )
```
